1024 devices in a mesh: tile: 64 (over z_hi, x, core), band: 8 (over y), chan: 2 (over z_lo).
Axes of the slice: x: 8, y: 8, z: 8 (z_hi: 4, z_lo: 2; z = z_hi * 2 + z_lo), core: 2. Of those that a mesh axis runs over, the one named last changes fastest.
Arguments:
- records: bfloat16 [262144, 128], P(('tile', 'band', 'chan')), may hold values from -6 to 6
- instrument: int32 [262144], P(('tile', 'band', 'chan')), may hold values from 0 to 7
- record_tile: int32 [262144, 1], P(('tile', 'band', 'chan')), may hold values from 0 to 63; in each aligned block of 256 rows (0 to 255, 256 to 511, ...) at most 8 rows name the same one
- record_cell: int32 [262144], P(('tile', 'band', 'chan')), may hold values from 0 to 1023
- inst_gain: float32 [8, 128], replicated, may hold values from 0.5 to 2
- inst_bias: float32 [8, 128], replicated, may hold values from -3 to 3
- embed_weight: bfloat16 [128, 256], P(None, 'chan'), may hold values from -0.5 to 0.5
- dens_weight: float32 [256], P('chan'), may hold values from -5 to 5
- embed_bias: float32 [256], P('chan'), may hold values from -3 to 3
- conv_weight: bfloat16 [2, 3, 3, 256, 256], P(None, None, None, None, 'chan'), may hold values from -0.125 to 0.125
- conv_bias: float32 [2, 256], P(None, 'chan'), may hold values from -3 to 3
Outputs:
- band_field: bfloat16 [64, 8, 1024, 256], P('tile', 'band', None, 'chan')
The draws below stay inside these ranges and needn't reach their ends.
Inputs may be any that keep to these rules, and one draw needn't show every extreme that they name: `record_tile`: among the 256 rows of one device no tile is named by more than 8 records, a bound that some block reaches.
All inputs are finite; a program needn't handle non-finite values.
Results may differ from the reference program's by a relative error of at most 0.0059.
Values may be sent and summed in bfloat16 or wider, within the bound.
A program may use at most 32 MiB of HBM per device.

```python
import math
import jax
import jax.numpy as jnp
import numpy as np
from jax import lax

RAD = 128
C = 256
NINST = 8
LAYERS = 2
LAT_DEV = 64
LON_DEV = 16
R_DEV = 256
CAP = 8
NREC = 262144
NLAT = 512
NLON = 1024
N_TILE = 64
N_BAND = 8
N_CHAN = 2


def set_ends(values, rng, low, high):
    shape = values.shape
    place = [jax.random.randint(jax.random.fold_in(rng, axis), (), 0, shape[axis]) for axis in range(len(shape))]
    values = values.at[tuple(place)].set(low)
    longest = shape.index(max(shape))
    place[longest] = (place[longest] + 1) % shape[longest]
    return values.at[tuple(place)].set(high)


def steps_of(own_key, shape, cuts, low, high):
    def one(axis_at, parts):
        draws = jax.random.uniform(jax.random.fold_in(jax.random.fold_in(own_key, 6), axis_at), (parts,), jnp.float32, low / len(cuts), high / len(cuts))
        return jnp.repeat(jnp.exp(draws), shape[axis_at] // parts).reshape((-1,) + (1,) * (len(shape) - axis_at - 1))

    loudness = one(*cuts[0])
    for cut in cuts[1:]:
        loudness = loudness * one(*cut)
    return loudness


def routed_block(own_key, own, number, rows, amount, top, most, lean):
    order = jax.random.permutation(own_key, amount)
    packed, usual = portions_of(amount, rows * top, most, lean, True), portions_of(amount, rows * top, most, lean, False)
    places = jnp.arange(amount)

    def named(sizes, offset_by):
        used = int((sizes > 0).sum())
        fixed = max(1, used // 4)
        moved = fixed + (places - fixed + offset_by * (used - fixed)) % max(1, amount - fixed)
        return jnp.zeros((amount,), jnp.int32).at[order[jnp.where(places < fixed, places, moved)]].set(jnp.asarray(sizes, jnp.int32))

    sizes = jnp.where(number % 4 == 0, named(packed, number // 4), named(usual, number - number // 4 - 1))
    mixed = jax.random.permutation(jax.random.fold_in(own, 3), amount)
    source_of, taker = mixed[0:amount // 2 * 2:2], mixed[1:amount // 2 * 2:2]
    margin = jnp.minimum(sizes[source_of] - 1, most - sizes[taker]) // 2
    margin = jnp.where((source_of == order[0]) | (taker == order[0]) | (sizes[taker] == 0), 0, jnp.maximum(margin, 0))
    moved = jax.random.randint(jax.random.fold_in(own, 4), (amount // 2,), 0, 1 << 20) % (margin + 1)
    sizes = sizes.at[source_of].add(-moved).at[taker].add(moved)
    members = jnp.searchsorted(jnp.cumsum(sizes), jnp.arange(rows * top), side="right").astype(jnp.int32)
    table = members.reshape(top, rows).T
    table = table[jax.random.permutation(jax.random.fold_in(own, 1), rows)]
    offset_by = jax.random.randint(jax.random.fold_in(own, 2), (rows, 1), 0, top)
    return jnp.take_along_axis(table, (jnp.arange(top)[None, :] + offset_by) % top, axis=1)


def portions_of(number_of, total, limit, lean, full):
    loads = [(1 << 20) // math.isqrt(standing ** lean) + 1 for standing in range(1, number_of + 1)]
    largest = limit if full else min(limit, max(-(-total // number_of), total * loads[0] // sum(loads)))
    least = 1 if total - largest >= number_of - 1 else 0
    given, spare = [largest] + [least] * (number_of - 1), total - largest - least * (number_of - 1)
    while spare > 0:
        candidates = [i for i in range(1, number_of) if given[i] < largest] or [i for i in range(1, number_of) if given[i] < limit]
        whole, budget = sum([loads[i] for i in candidates]), spare
        for i in candidates:
            extra = min(limit - given[i], max(1, budget * loads[i] // whole), spare)
            given[i] = given[i] + extra
            spare = spare - extra
    return np.array(given)


def normal_values(key, extent, deviation, most, pieces=(), kind=jnp.bfloat16):
    array = jax.random.normal(key, extent, jnp.float32) * deviation
    if len(pieces) > 0:
        array = steps_of(key, extent, pieces, -0.22, 0.18) * array
    return jnp.clip(array, min=-most, max=most).astype(kind)


def setup_inputs(seed: int = 0) -> dict:
    arg_keys = jax.random.split(jax.random.key(seed), 12)
    records = normal_values(arg_keys[0], (NREC, RAD), 1.0, 6.0, ((0, 1024),))
    instrument = set_ends(jax.random.randint(arg_keys[1], (NREC,), 0, NINST), jax.random.fold_in(arg_keys[1], 1), 0, NINST - 1).astype(jnp.int32)
    record_tile_keys = jax.random.split(jax.random.fold_in(arg_keys[2], 1), NREC // R_DEV)
    record_tile_turns = jax.random.permutation(jax.random.fold_in(arg_keys[2], 3), NREC // R_DEV)
    record_tile = jax.vmap(lambda own, number: routed_block(jax.random.fold_in(arg_keys[2], 2), own, number, R_DEV, N_TILE, 1, CAP, 2))(record_tile_keys, record_tile_turns).reshape((NREC, 1))
    record_cell = set_ends(jax.random.randint(arg_keys[3], (NREC,), 0, LAT_DEV * LON_DEV), jax.random.fold_in(arg_keys[3], 1), 0, (LAT_DEV * LON_DEV) - 1).astype(jnp.int32)
    inst_gain = jnp.clip(jnp.exp(jax.random.uniform(arg_keys[4], (NINST, RAD), jnp.float32, math.log(0.5), math.log(2.0))), 0.5, 2.0)
    inst_bias = normal_values(arg_keys[5], (NINST, RAD), 0.5, 3.0, (), jnp.float32)
    embed_weight = normal_values(arg_keys[6], (RAD, C), RAD ** -0.5, 0.5, ((1, 2),))
    dens_weight = normal_values(arg_keys[7], (C,), 1.0, 5.0, ((0, 2),), jnp.float32)
    embed_bias = normal_values(arg_keys[8], (C,), 0.5, 3.0, ((0, 2),), jnp.float32)
    conv_weight = normal_values(arg_keys[9], (LAYERS, 3, 3, C, C), (9 * C) ** -0.5, 0.125, ((4, 2),))
    conv_bias = normal_values(arg_keys[10], (LAYERS, C), 0.5, 3.0, ((1, 2),), jnp.float32)
    return dict(records=records, instrument=instrument, record_tile=record_tile, record_cell=record_cell, inst_gain=inst_gain, inst_bias=inst_bias, embed_weight=embed_weight, dens_weight=dens_weight, embed_bias=embed_bias, conv_weight=conv_weight, conv_bias=conv_bias)


def reference(records, instrument, record_tile, record_cell, inst_gain, inst_bias, embed_weight, dens_weight, embed_bias, conv_weight, conv_bias):
    corrected = (records.astype(jnp.float32) * inst_gain[instrument] + inst_bias[instrument]).astype(jnp.bfloat16)
    position = jnp.arange(NREC, dtype=jnp.int32)
    device_index = position // R_DEV
    band_index = (device_index // N_CHAN) % N_BAND
    lat_index = band_index * LAT_DEV + record_cell // LON_DEV
    lon_index = record_tile[:, 0] * LON_DEV + record_cell % LON_DEV
    flat_index = (lat_index * NLON + lon_index).astype(jnp.int32)
    cell_sum = jax.ops.segment_sum(corrected.astype(jnp.float32), flat_index, num_segments=NLAT * NLON)
    cell_count = jax.ops.segment_sum(jnp.ones((NREC,), jnp.float32), flat_index, num_segments=NLAT * NLON)
    averaged = (cell_sum / jnp.maximum(cell_count, 1.0)[:, None]).astype(jnp.bfloat16)
    density = cell_count / (cell_count + 1.0)
    grid_state = jnp.dot(averaged, embed_weight, preferred_element_type=jnp.float32)
    grid_state = grid_state + density[:, None] * dens_weight[None, :] + embed_bias[None, :]
    grid_state = grid_state.astype(jnp.bfloat16).reshape(NLAT, NLON, C)
    for layer_idx in range(LAYERS):
        padded = jnp.pad(grid_state, ((1, 1), (1, 1), (0, 0))).astype(jnp.float32)
        summed = lax.conv_general_dilated(padded[None], conv_weight[layer_idx].astype(jnp.float32), (1, 1), "VALID", dimension_numbers=("NHWC", "HWIO", "NHWC"), precision=lax.Precision.HIGHEST)[0]
        grid_state = (grid_state.astype(jnp.float32) + jax.nn.gelu(summed + conv_bias[layer_idx][None, None, :])).astype(jnp.bfloat16)
    return grid_state.reshape(N_BAND, LAT_DEV, NLON, C).transpose(1, 0, 2, 3)
```

```python
import functools
import math

import jax
import jax.numpy as jnp
from jax import lax
from jax.experimental import pallas as pl
from jax.experimental.pallas import tpu as pltpu
from jax.sharding import PartitionSpec as P

MESH = pl.DeviceIdType.MESH
F32, BF16, I32 = jnp.float32, jnp.bfloat16, jnp.int32
LAT_DEV, LON_DEV = 64, 16
HALF = LAT_DEV // 2
EXT = HALF + 4
EP = 48
CAP = 8
C = 256
SIDE = 2 * EP
MSG = 2 * SIDE + 32
NCELL = EXT * LON_DEV


def mm(a, b):
    return jnp.dot(a, b, preferred_element_type=F32)


def gelu(x):
    inner = math.sqrt(2.0 / math.pi) * (x + 0.044715 * (x * x * x))
    return 0.5 * x * (1.0 + jnp.tanh(inner))


def iotas(rows, cols):
    return lax.broadcasted_iota(I32, (rows, cols), 0), lax.broadcasted_iota(I32, (rows, cols), 1)


def onehot(mask):
    return jnp.where(mask, 1.0, 0.0).astype(BF16)


def thirds(x):
    a = x.astype(BF16).astype(F32)
    b = (x - a).astype(BF16).astype(F32)
    return [a, b, x - a - b]


def kernel(
    n_tile, n_band,
    rec, inst, rtile, rcell, gain, bias, ew, dw, eb, cw, cb,
    out,
    send, send_c, recv, recv_c, wh, ewh, small,
    field, cols, msg, rows, x3, xe, x3g, res,
    halo_sel, ins_sel, col_sel, own_sel,
    s_loc, s_rec, r_rec, s_cell, r_cell, s_cell2, r_cell2,
    s_par, r_par, s_w, r_w, s_w2, r_w2, s_halo, r_halo, s_out, r_out,
):
    t, b, c = lax.axis_index("tile"), lax.axis_index("band"), lax.axis_index("chan")
    oc = 1 - c
    west, east = lax.rem(t + n_tile - 1, n_tile), lax.rem(t + 1, n_tile)
    nb = lax.rem(b + n_band - 1 + 2 * c, n_band)
    core = lax.rem(t, 2)
    sibling = t + 1 - 2 * core
    zside = lax.rem(t + n_tile - 16 + 32 * c, n_tile)
    halo_to = ((west, nb), (t, nb), (east, nb))

    def dev(tt, bb, cc):
        return {"tile": tt, "band": bb, "chan": cc}

    def remote(src, dst, ss, rs, to):
        return pltpu.make_async_remote_copy(
            src_ref=src, dst_ref=dst, send_sem=ss, recv_sem=rs, device_id=to, device_id_type=MESH
        )

    barrier = pltpu.get_barrier_semaphore()

    def greet(tt, bb, cc):
        pl.semaphore_signal(barrier, inc=1, device_id=dev(tt, bb, cc), device_id_type=MESH)

    def greet_band(k, carry):
        d = lax.rem(t + k, n_tile)
        greet(d, b, c)
        greet(d, b, oc)
        return carry

    greet(t, b, oc)
    lax.fori_loop(1, n_tile, greet_band, 0)
    for tt, bb in halo_to:
        greet(tt, bb, oc)

    own_w = pltpu.make_async_copy(cw, wh.at[c], s_loc.at[0])
    own_w.start()

    n_inst = gain.shape[0]
    n_rec = rec.shape[0]
    q, _ = iotas(n_inst, n_rec)
    pick = jnp.where(q == inst[...], 1.0, 0.0)
    pick = jnp.concatenate([pick, pick, pick], axis=0).astype(BF16)
    table = jnp.concatenate(
        [jnp.concatenate(thirds(gain[...]), axis=0), jnp.concatenate(thirds(bias[...]), axis=0)],
        axis=1,
    ).astype(BF16)
    lines = lax.dot_general(pick, table, (((0,), (0,)), ((), ())), preferred_element_type=F32)
    fixed = (rec[...].astype(F32) * lines[:, :128] + lines[:, 128:]).astype(BF16)

    q, _ = iotas(n_tile, n_rec)
    hits = q == rtile[...]
    hits_f = jnp.where(hits, 1.0, 0.0)
    q, n = iotas(n_rec, n_rec)
    rank = jnp.sum(hits_f * mm(hits_f.astype(BF16), onehot(q <= n)), axis=0, keepdims=True) - 1.0
    rank = rank.astype(I32)
    slot = rtile[...] * CAP + rank
    q, _ = iotas(n_tile * CAP, n_rec)
    send[...] = mm(onehot(q == slot), fixed).astype(BF16).reshape(n_tile, CAP, 128)
    q, _ = iotas(128, n_rec)
    place = onehot(q == rank)
    cell = rcell[...]
    dims = (((1,), (1,)), ((), ()))
    high = lax.dot_general((hits_f * (cell // 32 + 16).astype(F32)).astype(BF16), place, dims, preferred_element_type=F32)
    low = lax.dot_general((hits_f * lax.rem(cell, 32).astype(F32)).astype(BF16), place, dims, preferred_element_type=F32)
    send_c[...] = (high * 32.0 + low).reshape(n_tile, 1, 128)

    ewh[c] = ew[...]
    small[c, 0:1] = dw[...]
    small[c, 1:2] = eb[...]
    small[c, 2:4] = cb[...]

    pl.semaphore_wait(barrier, 2 * n_tile - 1 + 3)

    def send_cells(k, carry):
        d = lax.rem(t + k, n_tile)
        remote(send_c.at[d], recv_c.at[c, k], s_cell, r_cell, dev(d, b, c)).start()
        return carry

    def send_rows(k, carry):
        d = lax.rem(t + k, n_tile)
        remote(send.at[d], recv.at[c, k], s_rec, r_rec, dev(d, b, c)).start()
        remote(send.at[d], recv.at[c, k], s_rec, r_rec, dev(d, b, oc)).start()
        return carry

    pltpu.make_async_copy(send_c.at[t], recv_c.at[c, 0], r_cell).start()
    pltpu.make_async_copy(send.at[t], recv.at[c, 0], r_rec).start()
    lax.fori_loop(1, n_tile, send_cells, 0)
    remote(send.at[t], recv.at[c, 0], s_rec, r_rec, dev(t, b, oc)).start()
    lax.fori_loop(1, n_tile, send_rows, 0)

    par = [
        remote(ewh.at[c], ewh.at[c], s_par.at[0], r_par.at[0], dev(t, b, oc)),
        remote(small.at[c], small.at[c], s_par.at[1], r_par.at[1], dev(t, b, oc)),
    ]
    for p in par:
        p.start()
    n_w = cw.shape[1]
    quarter = n_w // 4
    near = [pl.ds(pl.multiple_of((2 * core + s) * quarter, 16), quarter) for s in range(2)]
    half = pl.ds(pl.multiple_of(2 * core * quarter, 16), 2 * quarter)
    parts, shares = [], []
    for layer in range(2):
        for s, to in enumerate((dev(t, b, oc), dev(zside, b, oc))):
            i = 2 * layer + s
            parts.append(remote(cw.at[layer, near[s]], wh.at[c, layer, near[s]], s_w.at[i], r_w.at[i], to))
        shares.append(remote(wh.at[oc, layer, half], wh.at[oc, layer, half], s_w2.at[layer], r_w2.at[layer], dev(sibling, b, c)))
    parts[0].start()
    parts[1].start()

    first = 34 * c
    sent = 2 + 30 * c
    lat_ok = jnp.logical_not(jnp.logical_or(jnp.logical_and(b == 0, c == 0), jnp.logical_and(b == n_band - 1, c == 1)))
    lat_ok = lat_ok.astype(I32)
    west_ok = (t > 0).astype(I32)
    east_ok = (t < n_tile - 1).astype(I32)

    q, n = iotas(MSG, NCELL)
    edge = 16 * q + jnp.where(q < EP, 0, jnp.where(q < 2 * EP, 1 - 16 * EP, jnp.where(q < 3 * EP, 14 - 32 * EP, 15 - 48 * EP)))
    m = q - 2 * SIDE
    side = jnp.where(m >= 16, 1, 0)
    m = m - 16 * side
    col = jnp.where(m >= 2, 1, 0)
    corner = (sent + m - 2 * col) * 16 + 14 * side + col
    corner = jnp.where(m < 4, corner, -1)
    col_sel[...] = onehot(n == jnp.where(q < 2 * SIDE, edge, corner))

    q, n = iotas(2 * SIDE, MSG)
    group = jnp.where(q >= EP, 1, 0) + jnp.where(q >= 2 * EP, 1, 0) + jnp.where(q >= 3 * EP, 1, 0)
    e = q - EP * group
    outer = jnp.logical_and(e >= first, e < first + 2)
    corner = 2 * SIDE + jnp.where(group >= 2, 16, 0) + jnp.where(jnp.logical_or(group == 1, group == 3), 2, 0) + e - first
    ok = jnp.where(group >= 2, east_ok, west_ok) * jnp.where(outer, lat_ok, 1)
    target = jnp.where(outer, corner, q)
    target = jnp.where(jnp.logical_and(ok > 0, e < EXT), target, -1)
    halo_sel[...] = onehot(n == target)

    q, n = iotas(NCELL, SIDE)
    ins_sel[...] = onehot(q == jnp.where(n < EP, 16 * n, 16 * (n - EP) + 15))
    q, n = iotas(SIDE, NCELL)
    own_sel[...] = onehot(n == jnp.where(q < EP, 16 * q, 16 * (q - EP) + 15))

    pltpu.make_async_copy(recv_c.at[c], recv_c.at[c], r_cell).wait()
    forward = remote(recv_c.at[c], recv_c.at[c], s_cell2, r_cell2, dev(t, b, oc))
    forward.start()
    parts[0].wait_recv()
    parts[1].wait_recv()
    shares[0].start()
    parts[2].start()
    parts[3].start()
    forward.wait_recv()
    q, n = iotas(n_tile, n_tile * CAP)
    spread = onehot(jnp.logical_and(n >= q * CAP, n < q * CAP + CAP))
    q, n = iotas(CAP, n_tile * CAP)
    mine = q == lax.rem(n, CAP)
    ids = []
    for s in range(2):
        code = recv_c[s].reshape(n_tile, 128)[:, :128]
        high = jnp.floor(code * (1.0 / 32.0))
        low = code - 32.0 * high
        dims = (((0,), (0,)), ((), ()))
        h = lax.dot_general(high.astype(BF16), spread, dims, preferred_element_type=F32)[:CAP]
        lo = lax.dot_general(low.astype(BF16), spread, dims, preferred_element_type=F32)[:CAP]
        ids.append(jnp.sum(jnp.where(mine, h * 32.0 + lo, 0.0), axis=0, keepdims=True))
    ids = jnp.concatenate(ids, axis=1)
    q, _ = iotas(NCELL, 2 * n_tile * CAP)
    hot = onehot(q == ids.astype(I32) - (512 + 16 * (HALF * c - 2)))

    for p in par:
        p.wait_recv()
    pltpu.make_async_copy(recv, recv, r_rec).wait()

    values = recv[...].reshape(2 * n_tile * CAP, 128)
    sums = mm(hot, jnp.concatenate([values, jnp.ones_like(values)], axis=1))
    count = sums[:, 128:]
    averaged = (sums[:, :128] / jnp.maximum(count, 1.0)).astype(BF16)
    density = count / (count + 1.0)
    weights = jnp.concatenate([ewh[0], ewh[1]], axis=1)
    dens = jnp.concatenate([density * small[s, 0:1] + small[s, 1:2] for s in range(2)], axis=1)
    grid = (mm(averaged, weights) + dens).astype(BF16)
    field[...] = grid.reshape(EXT, LON_DEV, C)
    cols[...] = mm(col_sel[...], grid).astype(BF16)

    halo = [
        remote(field.at[pl.ds(sent, 2)], rows, s_halo.at[0], r_halo.at[0], dev(t, nb, oc)),
        remote(cols.at[pl.ds(0, SIDE)], msg.at[pl.ds(SIDE, SIDE)], s_halo.at[1], r_halo.at[1], dev(west, b, c)),
        remote(cols.at[pl.ds(SIDE, SIDE)], msg.at[pl.ds(0, SIDE)], s_halo.at[2], r_halo.at[2], dev(east, b, c)),
        remote(cols.at[pl.ds(2 * SIDE, 16)], msg.at[pl.ds(2 * SIDE + 16, 16)], s_halo.at[3], r_halo.at[3], dev(west, nb, oc)),
        remote(cols.at[pl.ds(2 * SIDE + 16, 16)], msg.at[pl.ds(2 * SIDE, 16)], s_halo.at[4], r_halo.at[4], dev(east, nb, oc)),
    ]
    for h in halo:
        h.start()
    parts[2].wait_recv()
    parts[3].wait_recv()
    shares[1].start()
    shares[0].wait_recv()
    own_w.wait()
    halo[0].wait()
    field[pl.ds(first, 2)] = (rows[...].astype(F32) * lat_ok.astype(F32)).astype(BF16)
    for h in halo[1:]:
        h.wait()

    def weight(layer, i):
        part = pl.ds(i * 3 * C, 3 * C)
        return jnp.concatenate([wh[0, layer, part], wh[1, layer, part]], axis=1)

    def conv_bias(layer):
        return jnp.concatenate([small[0, 2 + layer : 3 + layer], small[1, 2 + layer : 3 + layer]], axis=1)

    def shifted(flat, insert):
        count = flat.shape[0]
        lon = lax.rem(lax.broadcasted_iota(I32, flat.shape, 0), LON_DEV)
        left = jnp.where(lon == 0, insert, pltpu.roll(flat, 1, 0)).astype(BF16)
        right = jnp.where(lon == LON_DEV - 1, insert, pltpu.roll(flat, count - 1, 0)).astype(BF16)
        return left.reshape(-1, LON_DEV, C), right.reshape(-1, LON_DEV, C)

    edges = mm(halo_sel[...], msg[...])
    edges_b = edges.astype(BF16)
    whole = field[...].reshape(NCELL, C)
    own = mm(own_sel[...], whole).astype(BF16)
    insert = mm(ins_sel[...], edges_b[EP : 3 * EP])
    left, right = shifted(whole.astype(F32), insert)
    x3[:, :, 0:C] = left
    x3[:, :, C : 2 * C] = field[...]
    x3[:, :, 2 * C :] = right
    xe[0:EP, 0:C] = edges_b[0:EP]
    xe[0:EP, C : 2 * C] = edges_b[EP : 2 * EP]
    xe[0:EP, 2 * C :] = own[0:EP]
    xe[EP:, 0:C] = own[EP:]
    xe[EP:, C : 2 * C] = edges_b[2 * EP : 3 * EP]
    xe[EP:, 2 * C :] = edges_b[3 * EP :]

    top_bad = jnp.logical_and(b == 0, c == 0).astype(I32)
    low_bad = jnp.logical_and(b == n_band - 1, c == 1).astype(I32)
    y = [mm(xe[...], weight(0, i)) for i in range(3)]
    y = pltpu.roll(y[0], 1, 0) + y[1] + pltpu.roll(y[2], SIDE - 1, 0) + conv_bias(0)
    q, _ = iotas(SIDE, C)
    e = jnp.where(q >= EP, q - EP, q)
    ok = jnp.where(q >= EP, east_ok, west_ok)
    keep = jnp.logical_and(ok > 0, jnp.logical_and(e >= 1 + top_bad, e <= EXT - 2 - low_bad))
    edge_out = jnp.where(keep, edges[EP : 3 * EP] + gelu(y), 0.0).astype(BF16)

    n_out = EXT - 2
    y = mm(x3[0:n_out].reshape(n_out * LON_DEV, 3 * C), weight(0, 0))
    y = y + mm(x3[1 : n_out + 1].reshape(n_out * LON_DEV, 3 * C), weight(0, 1))
    y = y + mm(x3[2 : n_out + 2].reshape(n_out * LON_DEV, 3 * C), weight(0, 2))
    y = gelu(y + conv_bias(0)) + field[1 : n_out + 1].reshape(n_out * LON_DEV, C).astype(F32)
    q, _ = iotas(n_out * LON_DEV, C)
    keep = jnp.logical_and(q >= LON_DEV * top_bad, q < LON_DEV * (n_out - low_bad))
    y = jnp.where(keep, y, 0.0)
    yb = y.astype(BF16)
    insert = mm(ins_sel[LON_DEV : LON_DEV * (n_out + 1), :], edge_out)
    left, right = shifted(yb.astype(F32), insert)
    x3g[:, :, 0:C] = left
    x3g[:, :, C : 2 * C] = yb.reshape(n_out, LON_DEV, C)
    x3g[:, :, 2 * C :] = right

    shares[1].wait_recv()
    chunk = 8
    n_chunk = HALF // chunk
    here = (t // HALF) == c

    def step(g, carry):
        at = lax.rem(g + t // chunk, n_chunk) * chunk
        y = mm(x3g[pl.ds(at, chunk)].reshape(chunk * LON_DEV, 3 * C), weight(1, 0))
        y = y + mm(x3g[pl.ds(at + 1, chunk)].reshape(chunk * LON_DEV, 3 * C), weight(1, 1))
        y = y + mm(x3g[pl.ds(at + 2, chunk)].reshape(chunk * LON_DEV, 3 * C), weight(1, 2))
        base = x3g[pl.ds(at + 1, chunk), :, C : 2 * C].reshape(chunk * LON_DEV, C).astype(F32)
        y = (gelu(y + conv_bias(1)) + base).astype(BF16)
        for s in range(2):
            res[s, pl.ds(at, chunk)] = y[:, 128 * s : 128 * s + 128].reshape(chunk, LON_DEV, 128)

        def deliver(k, carry):
            r = at + lax.rem(k + t, chunk)
            d = HALF * c + r
            mine = out.at[pl.ds(pl.multiple_of(t * LON_DEV, LON_DEV), LON_DEV)]
            remote(res.at[oc, r], mine, s_out, r_out, dev(d, b, oc)).start()

            @pl.when(d != t)
            def _():
                remote(res.at[c, r], mine, s_out, r_out, dev(d, b, c)).start()

            @pl.when(d == t)
            def _():
                pltpu.make_async_copy(res.at[c, r], mine, r_out).start()

            return carry

        lax.fori_loop(0, chunk, deliver, 0)
        return carry

    lax.fori_loop(0, n_chunk, step, 0)

    def sent_bytes(ref, sem):
        pltpu.make_async_copy(ref, ref, sem).wait()

    sent_bytes(send_c.at[pl.ds(0, n_tile - 1)], s_cell)
    sent_bytes(recv.at[0], s_rec)
    sent_bytes(recv.at[0, pl.ds(0, n_tile - 1)], s_rec)
    forward.wait_send()
    for p in par + parts + shares:
        p.wait_send()
    n_lon = n_tile * LON_DEV
    pl.when(here)(lambda: sent_bytes(out.at[pl.ds(0, n_lon - LON_DEV)], s_out))
    pl.when(jnp.logical_not(here))(lambda: sent_bytes(out, s_out))
    sent_bytes(out, r_out)


def local(n_tile, n_band, records, instrument, record_tile, record_cell, inst_gain, inst_bias, embed_weight, dens_weight, embed_bias, conv_weight, conv_bias):
    n_rec = records.shape[0]
    vmem = pl.BlockSpec(memory_space=pltpu.VMEM)
    hbm = pl.BlockSpec(memory_space=pl.ANY)
    dma, scratch = pltpu.SemaphoreType.DMA, pltpu.VMEM
    taps = 9 * C
    result = pl.pallas_call(
        functools.partial(kernel, n_tile, n_band),
        out_shape=jax.ShapeDtypeStruct((n_tile * LON_DEV, 128), BF16),
        in_specs=[vmem] * 9 + [hbm, vmem],
        out_specs=vmem,
        scratch_shapes=[
            scratch((n_tile, CAP, 128), BF16),
            scratch((n_tile, 1, 128), F32),
            scratch((2, n_tile, CAP, 128), BF16),
            scratch((2, n_tile, 1, 128), F32),
            scratch((2, 2, taps, 128), BF16),
            scratch((2, 128, 128), BF16),
            scratch((2, 8, 128), F32),
            scratch((EXT, LON_DEV, C), BF16),
            scratch((MSG, C), BF16),
            scratch((MSG, C), BF16),
            scratch((2, LON_DEV, C), BF16),
            scratch((EXT, LON_DEV, 3 * C), BF16),
            scratch((SIDE, 3 * C), BF16),
            scratch((EXT - 2, LON_DEV, 3 * C), BF16),
            scratch((2, HALF, LON_DEV, 128), BF16),
            scratch((2 * SIDE, MSG), BF16),
            scratch((NCELL, SIDE), BF16),
            scratch((MSG, NCELL), BF16),
            scratch((SIDE, NCELL), BF16),
            dma((1,)), dma, dma, dma, dma, dma, dma,
            dma((2,)), dma((2,)), dma((4,)), dma((4,)), dma((2,)), dma((2,)), dma((5,)), dma((5,)), dma, dma,
        ],
        compiler_params=pltpu.CompilerParams(
            collective_id=0, has_side_effects=True, vmem_limit_bytes=48 * 1024 * 1024
        ),
        name="encode",
    )(
        records,
        instrument.reshape(1, n_rec),
        record_tile.reshape(1, n_rec),
        record_cell.reshape(1, n_rec),
        inst_gain,
        inst_bias,
        embed_weight,
        dens_weight.reshape(1, -1),
        embed_bias.reshape(1, -1),
        conv_weight.reshape(2, taps, -1),
        conv_bias,
    )
    return result[None, None]


def solution(mesh):
    in_specs = (
        P(("tile", "band", "chan"), None),
        P(("tile", "band", "chan")),
        P(("tile", "band", "chan"), None),
        P(("tile", "band", "chan")),
        P(),
        P(),
        P(None, "chan"),
        P("chan"),
        P("chan"),
        P(None, None, None, None, "chan"),
        P(None, "chan"),
    )
    return jax.shard_map(
        functools.partial(local, mesh.shape["tile"], mesh.shape["band"]),
        mesh=mesh,
        in_specs=in_specs,
        out_specs=P("tile", "band", None, "chan"),
        check_vma=False,
    )
```

```python
import functools
import math

import jax
import jax.numpy as jnp
from jax import lax
from jax.experimental import pallas as pl
from jax.experimental.pallas import tpu as pltpu
from jax.sharding import PartitionSpec as P

MESH = pl.DeviceIdType.MESH
F32, BF16, I32 = jnp.float32, jnp.bfloat16, jnp.int32
LAT_DEV, LON_DEV = 64, 16
HALF = LAT_DEV // 2
EXT = HALF + 4
EP = 48
CAP = 8
C = 256
SIDE = 2 * EP
MSG = 2 * SIDE + 32
NCELL = EXT * LON_DEV


def mm(a, b):
    return jnp.dot(a, b, preferred_element_type=F32)


def gelu(x):
    inner = math.sqrt(2.0 / math.pi) * (x + 0.044715 * (x * x * x))
    return 0.5 * x * (1.0 + jnp.tanh(inner))


def iotas(rows, cols):
    return lax.broadcasted_iota(I32, (rows, cols), 0), lax.broadcasted_iota(I32, (rows, cols), 1)


def onehot(mask):
    return jnp.where(mask, 1.0, 0.0).astype(BF16)


def thirds(x):
    a = x.astype(BF16).astype(F32)
    b = (x - a).astype(BF16).astype(F32)
    return [a, b, x - a - b]


def kernel(
    n_tile, n_band,
    rec_in, inst_in, rtile_in, rcell_in, gain_in, bias_in, ew_in, dw_in, eb_in, cw, cb_in,
    out,
    rec, inst, rtile, rcell, gain, bias, dw, eb, cb,
    send, send_c, recv, recv_c, wh, ewh, small,
    field, cols, msg, rows, x3, xe, x3g, res,
    halo_sel, ins_sel, col_sel, own_sel,
    s_loc, s_rec, r_rec, s_cell, r_cell, s_cell2, r_cell2,
    s_par, r_par, s_w, r_w, s_w2, r_w2, s_halo, r_halo, s_out, r_out,
):
    t, b, c = lax.axis_index("tile"), lax.axis_index("band"), lax.axis_index("chan")
    oc = 1 - c
    west, east = lax.rem(t + n_tile - 1, n_tile), lax.rem(t + 1, n_tile)
    nb = lax.rem(b + n_band - 1 + 2 * c, n_band)
    core = lax.rem(t, 2)
    sibling = t + 1 - 2 * core
    zside = lax.rem(t + n_tile - 16 + 32 * c, n_tile)
    halo_to = ((west, nb), (t, nb), (east, nb))

    def dev(tt, bb, cc):
        return {"tile": tt, "band": bb, "chan": cc}

    def remote(src, dst, ss, rs, to):
        return pltpu.make_async_remote_copy(
            src_ref=src, dst_ref=dst, send_sem=ss, recv_sem=rs, device_id=to, device_id_type=MESH
        )

    taken = [
        pltpu.make_async_copy(src, dst, s_loc.at[i])
        for i, (src, dst) in enumerate(
            [
                (rtile_in, rtile), (rcell_in, rcell), (inst_in, inst), (gain_in, gain), (bias_in, bias), (rec_in, rec),
                (dw_in, dw), (eb_in, eb), (cb_in, cb), (ew_in, ewh.at[c]), (cw, wh.at[c]),
            ]
        )
    ]
    for copy in taken:
        copy.start()
    own_w = taken[-1]

    barrier = pltpu.get_barrier_semaphore()

    def greet(tt, bb, cc):
        pl.semaphore_signal(barrier, inc=1, device_id=dev(tt, bb, cc), device_id_type=MESH)

    plane = 16
    z_at, in_plane = t // plane, lax.rem(t, plane)
    x_at = in_plane // 2

    def far_first(k):
        j, dc = k // 2, lax.rem(k, 2)
        turn, j = j // 8, lax.rem(j, 8)
        n_z = n_tile // plane
        dz = lax.rem(n_z // 2 + (1 - 2 * lax.rem(turn, 2)) * ((turn + 1) // 2) + n_z, n_z)
        dx = lax.rem(4 + (1 - 2 * lax.rem(j, 2)) * ((j + 1) // 2) + 8, 8)
        dc = 1 - dc
        d = lax.rem(z_at + dz, n_z) * plane + lax.rem(x_at + dx, 8) * 2 + lax.rem(core + dc, 2)
        return d, (dz * 8 + dx) * 2 + dc

    def greet_band(k, carry):
        d, _ = far_first(k)
        greet(d, b, c)
        greet(d, b, oc)
        return carry

    lax.fori_loop(0, n_tile - 1, greet_band, 0)
    for tt, bb in halo_to:
        greet(tt, bb, oc)
    greet(t, b, oc)


    for copy in taken[:-1]:
        copy.wait()

    n_inst = gain.shape[0]
    n_rec = rec.shape[0]
    q, _ = iotas(n_inst, n_rec)
    pick = jnp.where(q == inst[...], 1.0, 0.0)
    pick = jnp.concatenate([pick, pick, pick], axis=0).astype(BF16)
    table = jnp.concatenate(
        [jnp.concatenate(thirds(gain[...]), axis=0), jnp.concatenate(thirds(bias[...]), axis=0)],
        axis=1,
    ).astype(BF16)
    lines = lax.dot_general(pick, table, (((0,), (0,)), ((), ())), preferred_element_type=F32)
    fixed = (rec[...].astype(F32) * lines[:, :128] + lines[:, 128:]).astype(BF16)

    q, _ = iotas(n_tile, n_rec)
    hits = q == rtile[...]
    hits_f = jnp.where(hits, 1.0, 0.0)
    q, n = iotas(n_rec, n_rec)
    rank = jnp.sum(hits_f * mm(hits_f.astype(BF16), onehot(q <= n)), axis=0, keepdims=True) - 1.0
    rank = rank.astype(I32)
    slot = rtile[...] * CAP + rank
    q, _ = iotas(n_tile * CAP, n_rec)
    send[...] = mm(onehot(q == slot), fixed).astype(BF16).reshape(n_tile, CAP, 128)
    q, _ = iotas(128, n_rec)
    place = onehot(q == rank)
    cell = rcell[...]
    dims = (((1,), (1,)), ((), ()))
    high = lax.dot_general((hits_f * (cell // 32 + 16).astype(F32)).astype(BF16), place, dims, preferred_element_type=F32)
    low = lax.dot_general((hits_f * lax.rem(cell, 32).astype(F32)).astype(BF16), place, dims, preferred_element_type=F32)
    send_c[...] = (high * 32.0 + low).reshape(n_tile, 1, 128)

    small[c, 0:1] = dw[...]
    small[c, 1:2] = eb[...]
    small[c, 2:4] = cb[...]

    pl.semaphore_wait(barrier, 2 * n_tile - 1 + 3)

    def send_cells(i, carry):
        d, k = far_first(i)
        remote(send_c.at[d], recv_c.at[c, k], s_cell, r_cell, dev(d, b, c)).start()
        return carry

    def send_rows(i, carry):
        d, k = far_first(i)
        remote(send.at[d], recv.at[c, k], s_rec, r_rec, dev(d, b, c)).start()
        remote(send.at[d], recv.at[c, k], s_rec, r_rec, dev(d, b, oc)).start()
        return carry

    pltpu.make_async_copy(send_c.at[t], recv_c.at[c, 0], r_cell).start()
    pltpu.make_async_copy(send.at[t], recv.at[c, 0], r_rec).start()
    lax.fori_loop(0, n_tile - 1, send_cells, 0)
    lax.fori_loop(0, n_tile - 1, send_rows, 0)
    remote(send.at[t], recv.at[c, 0], s_rec, r_rec, dev(t, b, oc)).start()

    par = [
        remote(ewh.at[c], ewh.at[c], s_par.at[0], r_par.at[0], dev(t, b, oc)),
        remote(small.at[c], small.at[c], s_par.at[1], r_par.at[1], dev(t, b, oc)),
    ]
    for p in par:
        p.start()
    n_w = cw.shape[1]
    quarter = n_w // 4
    near = [pl.ds(pl.multiple_of((2 * core + s) * quarter, 16), quarter) for s in range(2)]
    half = pl.ds(pl.multiple_of(2 * core * quarter, 16), 2 * quarter)
    parts, shares = [], []
    for layer in range(2):
        for s, to in enumerate((dev(t, b, oc), dev(zside, b, oc))):
            i = 2 * layer + s
            parts.append(remote(cw.at[layer, near[s]], wh.at[c, layer, near[s]], s_w.at[i], r_w.at[i], to))
        shares.append(remote(wh.at[oc, layer, half], wh.at[oc, layer, half], s_w2.at[layer], r_w2.at[layer], dev(sibling, b, c)))
    parts[0].start()
    parts[1].start()

    first = 34 * c
    sent = 2 + 30 * c
    lat_ok = jnp.logical_not(jnp.logical_or(jnp.logical_and(b == 0, c == 0), jnp.logical_and(b == n_band - 1, c == 1)))
    lat_ok = lat_ok.astype(I32)
    west_ok = (t > 0).astype(I32)
    east_ok = (t < n_tile - 1).astype(I32)

    q, n = iotas(MSG, NCELL)
    edge = 16 * q + jnp.where(q < EP, 0, jnp.where(q < 2 * EP, 1 - 16 * EP, jnp.where(q < 3 * EP, 14 - 32 * EP, 15 - 48 * EP)))
    m = q - 2 * SIDE
    side = jnp.where(m >= 16, 1, 0)
    m = m - 16 * side
    col = jnp.where(m >= 2, 1, 0)
    corner = (sent + m - 2 * col) * 16 + 14 * side + col
    corner = jnp.where(m < 4, corner, -1)
    col_sel[...] = onehot(n == jnp.where(q < 2 * SIDE, edge, corner))

    q, n = iotas(2 * SIDE, MSG)
    group = jnp.where(q >= EP, 1, 0) + jnp.where(q >= 2 * EP, 1, 0) + jnp.where(q >= 3 * EP, 1, 0)
    e = q - EP * group
    outer = jnp.logical_and(e >= first, e < first + 2)
    corner = 2 * SIDE + jnp.where(group >= 2, 16, 0) + jnp.where(jnp.logical_or(group == 1, group == 3), 2, 0) + e - first
    ok = jnp.where(group >= 2, east_ok, west_ok) * jnp.where(outer, lat_ok, 1)
    target = jnp.where(outer, corner, q)
    target = jnp.where(jnp.logical_and(ok > 0, e < EXT), target, -1)
    halo_sel[...] = onehot(n == target)

    q, n = iotas(NCELL, SIDE)
    ins_sel[...] = onehot(q == jnp.where(n < EP, 16 * n, 16 * (n - EP) + 15))
    q, n = iotas(SIDE, NCELL)
    own_sel[...] = onehot(n == jnp.where(q < EP, 16 * q, 16 * (q - EP) + 15))

    pltpu.make_async_copy(recv_c.at[c], recv_c.at[c], r_cell).wait()
    forward = remote(recv_c.at[c], recv_c.at[c], s_cell2, r_cell2, dev(t, b, oc))
    forward.start()
    parts[0].wait_recv()
    parts[1].wait_recv()
    shares[0].start()
    parts[2].start()
    parts[3].start()
    forward.wait_recv()
    q, n = iotas(n_tile, n_tile * CAP)
    spread = onehot(jnp.logical_and(n >= q * CAP, n < q * CAP + CAP))
    q, n = iotas(CAP, n_tile * CAP)
    mine = q == lax.rem(n, CAP)
    ids = []
    for s in range(2):
        code = recv_c[s].reshape(n_tile, 128)[:, :128]
        high = jnp.floor(code * (1.0 / 32.0))
        low = code - 32.0 * high
        dims = (((0,), (0,)), ((), ()))
        h = lax.dot_general(high.astype(BF16), spread, dims, preferred_element_type=F32)[:CAP]
        lo = lax.dot_general(low.astype(BF16), spread, dims, preferred_element_type=F32)[:CAP]
        ids.append(jnp.sum(jnp.where(mine, h * 32.0 + lo, 0.0), axis=0, keepdims=True))
    ids = jnp.concatenate(ids, axis=1)
    q, _ = iotas(NCELL, 2 * n_tile * CAP)
    hot = onehot(q == ids.astype(I32) - (512 + 16 * (HALF * c - 2)))

    for p in par:
        p.wait_recv()
    pltpu.make_async_copy(recv, recv, r_rec).wait()

    values = recv[...].reshape(2 * n_tile * CAP, 128)
    sums = mm(hot, jnp.concatenate([values, jnp.ones_like(values)], axis=1))
    count = sums[:, 128:]
    averaged = (sums[:, :128] / jnp.maximum(count, 1.0)).astype(BF16)
    density = count / (count + 1.0)
    weights = jnp.concatenate([ewh[0], ewh[1]], axis=1)
    dens = jnp.concatenate([density * small[s, 0:1] + small[s, 1:2] for s in range(2)], axis=1)
    grid = (mm(averaged, weights) + dens).astype(BF16)
    field[...] = grid.reshape(EXT, LON_DEV, C)
    cols[...] = mm(col_sel[...], grid).astype(BF16)

    halo = [
        remote(field.at[pl.ds(sent, 2)], rows, s_halo.at[0], r_halo.at[0], dev(t, nb, oc)),
        remote(cols.at[pl.ds(0, SIDE)], msg.at[pl.ds(SIDE, SIDE)], s_halo.at[1], r_halo.at[1], dev(west, b, c)),
        remote(cols.at[pl.ds(SIDE, SIDE)], msg.at[pl.ds(0, SIDE)], s_halo.at[2], r_halo.at[2], dev(east, b, c)),
        remote(cols.at[pl.ds(2 * SIDE, 16)], msg.at[pl.ds(2 * SIDE + 16, 16)], s_halo.at[3], r_halo.at[3], dev(west, nb, oc)),
        remote(cols.at[pl.ds(2 * SIDE + 16, 16)], msg.at[pl.ds(2 * SIDE, 16)], s_halo.at[4], r_halo.at[4], dev(east, nb, oc)),
    ]
    for h in halo:
        h.start()
    parts[2].wait_recv()
    parts[3].wait_recv()
    shares[1].start()
    shares[0].wait_recv()
    own_w.wait()
    halo[0].wait()
    field[pl.ds(first, 2)] = (rows[...].astype(F32) * lat_ok.astype(F32)).astype(BF16)
    for h in halo[1:]:
        h.wait()

    def weight(layer, i):
        part = pl.ds(i * 3 * C, 3 * C)
        return jnp.concatenate([wh[0, layer, part], wh[1, layer, part]], axis=1)

    def conv_bias(layer):
        return jnp.concatenate([small[0, 2 + layer : 3 + layer], small[1, 2 + layer : 3 + layer]], axis=1)

    def shifted(flat, insert):
        count = flat.shape[0]
        lon = lax.rem(lax.broadcasted_iota(I32, flat.shape, 0), LON_DEV)
        left = jnp.where(lon == 0, insert, pltpu.roll(flat, 1, 0)).astype(BF16)
        right = jnp.where(lon == LON_DEV - 1, insert, pltpu.roll(flat, count - 1, 0)).astype(BF16)
        return left.reshape(-1, LON_DEV, C), right.reshape(-1, LON_DEV, C)

    edges = mm(halo_sel[...], msg[...])
    edges_b = edges.astype(BF16)
    whole = field[...].reshape(NCELL, C)
    own = mm(own_sel[...], whole).astype(BF16)
    insert = mm(ins_sel[...], edges_b[EP : 3 * EP])
    left, right = shifted(whole.astype(F32), insert)
    x3[:, :, 0:C] = left
    x3[:, :, C : 2 * C] = field[...]
    x3[:, :, 2 * C :] = right
    xe[0:EP, 0:C] = edges_b[0:EP]
    xe[0:EP, C : 2 * C] = edges_b[EP : 2 * EP]
    xe[0:EP, 2 * C :] = own[0:EP]
    xe[EP:, 0:C] = own[EP:]
    xe[EP:, C : 2 * C] = edges_b[2 * EP : 3 * EP]
    xe[EP:, 2 * C :] = edges_b[3 * EP :]

    top_bad = jnp.logical_and(b == 0, c == 0).astype(I32)
    low_bad = jnp.logical_and(b == n_band - 1, c == 1).astype(I32)
    y = [mm(xe[...], weight(0, i)) for i in range(3)]
    y = pltpu.roll(y[0], 1, 0) + y[1] + pltpu.roll(y[2], SIDE - 1, 0) + conv_bias(0)
    q, _ = iotas(SIDE, C)
    e = jnp.where(q >= EP, q - EP, q)
    ok = jnp.where(q >= EP, east_ok, west_ok)
    keep = jnp.logical_and(ok > 0, jnp.logical_and(e >= 1 + top_bad, e <= EXT - 2 - low_bad))
    edge_out = jnp.where(keep, edges[EP : 3 * EP] + gelu(y), 0.0).astype(BF16)

    n_out = EXT - 2
    y = mm(x3[0:n_out].reshape(n_out * LON_DEV, 3 * C), weight(0, 0))
    y = y + mm(x3[1 : n_out + 1].reshape(n_out * LON_DEV, 3 * C), weight(0, 1))
    y = y + mm(x3[2 : n_out + 2].reshape(n_out * LON_DEV, 3 * C), weight(0, 2))
    y = gelu(y + conv_bias(0)) + field[1 : n_out + 1].reshape(n_out * LON_DEV, C).astype(F32)
    q, _ = iotas(n_out * LON_DEV, C)
    keep = jnp.logical_and(q >= LON_DEV * top_bad, q < LON_DEV * (n_out - low_bad))
    y = jnp.where(keep, y, 0.0)
    yb = y.astype(BF16)
    insert = mm(ins_sel[LON_DEV : LON_DEV * (n_out + 1), :], edge_out)
    left, right = shifted(yb.astype(F32), insert)
    x3g[:, :, 0:C] = left
    x3g[:, :, C : 2 * C] = yb.reshape(n_out, LON_DEV, C)
    x3g[:, :, 2 * C :] = right

    shares[1].wait_recv()
    chunk = 8
    n_chunk = HALF // chunk
    here = (t // HALF) == c

    def step(g, carry):
        far_z = jnp.where(c == 0, jnp.where(z_at == 1, 0, jnp.where(z_at == 3, 1, jnp.where(z_at == 0, 1, 0))), jnp.where(z_at == 3, 0, jnp.where(z_at == 1, 1, jnp.where(z_at == 2, 1, 0))))
        zz = lax.rem(far_z + g // 2, 2)
        at = (zz * 2 + lax.rem(x_at // 4 + 1 + g, 2)) * chunk
        y = mm(x3g[pl.ds(at, chunk)].reshape(chunk * LON_DEV, 3 * C), weight(1, 0))
        y = y + mm(x3g[pl.ds(at + 1, chunk)].reshape(chunk * LON_DEV, 3 * C), weight(1, 1))
        y = y + mm(x3g[pl.ds(at + 2, chunk)].reshape(chunk * LON_DEV, 3 * C), weight(1, 2))
        base = x3g[pl.ds(at + 1, chunk), :, C : 2 * C].reshape(chunk * LON_DEV, C).astype(F32)
        y = (gelu(y + conv_bias(1)) + base).astype(BF16)
        for s in range(2):
            res[s, pl.ds(at, chunk)] = y[:, 128 * s : 128 * s + 128].reshape(chunk, LON_DEV, 128)

        def deliver(k, carry):
            r = at + lax.rem(k + t, chunk)
            d = HALF * c + r
            mine = out.at[pl.ds(pl.multiple_of(t * LON_DEV, LON_DEV), LON_DEV)]
            remote(res.at[oc, r], mine, s_out, r_out, dev(d, b, oc)).start()

            @pl.when(d != t)
            def _():
                remote(res.at[c, r], mine, s_out, r_out, dev(d, b, c)).start()

            @pl.when(d == t)
            def _():
                pltpu.make_async_copy(res.at[c, r], mine, r_out).start()

            return carry

        lax.fori_loop(0, chunk, deliver, 0)
        return carry

    lax.fori_loop(0, n_chunk, step, 0)

    def sent_bytes(ref, sem):
        pltpu.make_async_copy(ref, ref, sem).wait()

    sent_bytes(send_c.at[pl.ds(0, n_tile - 1)], s_cell)
    sent_bytes(recv.at[0], s_rec)
    sent_bytes(recv.at[0, pl.ds(0, n_tile - 1)], s_rec)
    forward.wait_send()
    for p in par + parts + shares:
        p.wait_send()
    n_lon = n_tile * LON_DEV
    pl.when(here)(lambda: sent_bytes(out.at[pl.ds(0, n_lon - LON_DEV)], s_out))
    pl.when(jnp.logical_not(here))(lambda: sent_bytes(out, s_out))
    sent_bytes(out, r_out)


def local(n_tile, n_band, records, instrument, record_tile, record_cell, inst_gain, inst_bias, embed_weight, dens_weight, embed_bias, conv_weight, conv_bias):
    n_rec = records.shape[0]
    hbm = pl.BlockSpec(memory_space=pltpu.HBM)
    dma, scratch = pltpu.SemaphoreType.DMA, pltpu.VMEM
    taps = 9 * C
    result = pl.pallas_call(
        functools.partial(kernel, n_tile, n_band),
        out_shape=jax.ShapeDtypeStruct((n_tile * LON_DEV, 128), BF16),
        in_specs=[hbm] * 11,
        out_specs=hbm,
        scratch_shapes=[
            scratch((n_rec, 128), BF16),
            scratch((1, n_rec), I32),
            scratch((1, n_rec), I32),
            scratch((1, n_rec), I32),
            scratch(inst_gain.shape, F32),
            scratch(inst_gain.shape, F32),
            scratch((1, 128), F32),
            scratch((1, 128), F32),
            scratch((2, 128), F32),
            scratch((n_tile, CAP, 128), BF16),
            scratch((n_tile, 1, 128), F32),
            scratch((2, n_tile, CAP, 128), BF16),
            scratch((2, n_tile, 1, 128), F32),
            scratch((2, 2, taps, 128), BF16),
            scratch((2, 128, 128), BF16),
            scratch((2, 8, 128), F32),
            scratch((EXT, LON_DEV, C), BF16),
            scratch((MSG, C), BF16),
            scratch((MSG, C), BF16),
            scratch((2, LON_DEV, C), BF16),
            scratch((EXT, LON_DEV, 3 * C), BF16),
            scratch((SIDE, 3 * C), BF16),
            scratch((EXT - 2, LON_DEV, 3 * C), BF16),
            scratch((2, HALF, LON_DEV, 128), BF16),
            scratch((2 * SIDE, MSG), BF16),
            scratch((NCELL, SIDE), BF16),
            scratch((MSG, NCELL), BF16),
            scratch((SIDE, NCELL), BF16),
            dma((11,)), dma, dma, dma, dma, dma, dma,
            dma((2,)), dma((2,)), dma((4,)), dma((4,)), dma((2,)), dma((2,)), dma((5,)), dma((5,)), dma, dma,
        ],
        compiler_params=pltpu.CompilerParams(
            collective_id=0, has_side_effects=True, vmem_limit_bytes=62 * 1024 * 1024
        ),
        name="encode",
    )(
        records,
        instrument.reshape(1, n_rec),
        record_tile.reshape(1, n_rec),
        record_cell.reshape(1, n_rec),
        inst_gain,
        inst_bias,
        embed_weight,
        dens_weight.reshape(1, -1),
        embed_bias.reshape(1, -1),
        conv_weight.reshape(2, taps, -1),
        conv_bias,
    )
    return result[None, None]


def solution(mesh):
    in_specs = (
        P(("tile", "band", "chan"), None),
        P(("tile", "band", "chan")),
        P(("tile", "band", "chan"), None),
        P(("tile", "band", "chan")),
        P(),
        P(),
        P(None, "chan"),
        P("chan"),
        P("chan"),
        P(None, None, None, None, "chan"),
        P(None, "chan"),
    )
    return jax.shard_map(
        functools.partial(local, mesh.shape["tile"], mesh.shape["band"]),
        mesh=mesh,
        in_specs=in_specs,
        out_specs=P("tile", "band", None, "chan"),
        check_vma=False,
    )
```

```python
import functools
import math

import jax
import jax.numpy as jnp
from jax import lax
from jax.experimental import pallas as pl
from jax.experimental.pallas import tpu as pltpu
from jax.sharding import PartitionSpec as P

MESH = pl.DeviceIdType.MESH
F32, BF16, I32 = jnp.float32, jnp.bfloat16, jnp.int32
LAT_DEV, LON_DEV = 64, 16
HALF = LAT_DEV // 2
EXT = HALF + 4
EP = 48
CAP = 8
C = 256
SIDE = 2 * EP
MSG = 2 * SIDE + 32
NCELL = EXT * LON_DEV


def mm(a, b):
    return jnp.dot(a, b, preferred_element_type=F32)


def gelu(x):
    inner = math.sqrt(2.0 / math.pi) * (x + 0.044715 * (x * x * x))
    return 0.5 * x * (1.0 + jnp.tanh(inner))


def iotas(rows, cols):
    return lax.broadcasted_iota(I32, (rows, cols), 0), lax.broadcasted_iota(I32, (rows, cols), 1)


def onehot(mask):
    return jnp.where(mask, 1.0, 0.0).astype(BF16)


def thirds(x):
    a = x.astype(BF16).astype(F32)
    b = (x - a).astype(BF16).astype(F32)
    return [a, b, x - a - b]


def kernel(
    n_tile, n_band,
    rec_in, inst_in, rtile_in, rcell_in, gain_in, bias_in, ew_in, dw_in, eb_in, cw, cb_in,
    out,
    rec, inst, rtile, rcell, gain, bias, dw, eb, cb,
    send, send_c, recv, recv_c, wh, ewh, small,
    field, cols, msg, rows, x3, xe, x3g, res,
    halo_sel, ins_sel, col_sel, own_sel,
    s_loc, s_rec, r_rec, s_cell, r_cell, s_cell2, r_cell2,
    s_par, r_par, s_w, r_w, s_w2, r_w2, s_halo, r_halo, s_out, r_out,
):
    t, b, c = lax.axis_index("tile"), lax.axis_index("band"), lax.axis_index("chan")
    oc = 1 - c
    west, east = lax.rem(t + n_tile - 1, n_tile), lax.rem(t + 1, n_tile)
    nb = lax.rem(b + n_band - 1 + 2 * c, n_band)
    core = lax.rem(t, 2)
    sibling = t + 1 - 2 * core
    zside = lax.rem(t + n_tile - 16 + 32 * c, n_tile)
    halo_to = ((west, nb), (t, nb), (east, nb))

    def dev(tt, bb, cc):
        return {"tile": tt, "band": bb, "chan": cc}

    def remote(src, dst, ss, rs, to):
        return pltpu.make_async_remote_copy(
            src_ref=src, dst_ref=dst, send_sem=ss, recv_sem=rs, device_id=to, device_id_type=MESH
        )

    taken = [
        pltpu.make_async_copy(src, dst, s_loc.at[i])
        for i, (src, dst) in enumerate(
            [
                (rtile_in, rtile), (rcell_in, rcell), (inst_in, inst), (gain_in, gain), (bias_in, bias), (rec_in, rec),
                (dw_in, dw), (eb_in, eb), (cb_in, cb), (ew_in, ewh.at[c]), (cw, wh.at[c]),
            ]
        )
    ]
    for copy in taken:
        copy.start()
    own_w = taken[-1]

    barrier = pltpu.get_barrier_semaphore()

    def greet(tt, bb, cc):
        pl.semaphore_signal(barrier, inc=1, device_id=dev(tt, bb, cc), device_id_type=MESH)

    plane = 16
    z_at, in_plane = t // plane, lax.rem(t, plane)
    x_at = in_plane // 2

    def far_first(k):
        j, dc = k // 2, lax.rem(k, 2)
        turn, j = j // 8, lax.rem(j, 8)
        n_z = n_tile // plane
        dz = lax.rem(n_z // 2 + (1 - 2 * lax.rem(turn, 2)) * ((turn + 1) // 2) + n_z, n_z)
        dx = lax.rem(4 + (1 - 2 * lax.rem(j, 2)) * ((j + 1) // 2) + 8, 8)
        dc = 1 - dc
        d = lax.rem(z_at + dz, n_z) * plane + lax.rem(x_at + dx, 8) * 2 + lax.rem(core + dc, 2)
        return d, (dz * 8 + dx) * 2 + dc

    def greet_band(k, carry):
        d, _ = far_first(k)
        greet(d, b, c)
        greet(d, b, oc)
        return carry

    lax.fori_loop(0, n_tile - 1, greet_band, 0)
    for tt, bb in halo_to:
        greet(tt, bb, oc)
    greet(t, b, oc)


    for copy in taken[:-1]:
        copy.wait()

    n_inst = gain.shape[0]
    n_rec = rec.shape[0]
    q, _ = iotas(n_inst, n_rec)
    pick = jnp.where(q == inst[...], 1.0, 0.0)
    pick = jnp.concatenate([pick, pick, pick], axis=0).astype(BF16)
    table = jnp.concatenate(
        [jnp.concatenate(thirds(gain[...]), axis=0), jnp.concatenate(thirds(bias[...]), axis=0)],
        axis=1,
    ).astype(BF16)
    lines = lax.dot_general(pick, table, (((0,), (0,)), ((), ())), preferred_element_type=F32)
    fixed = (rec[...].astype(F32) * lines[:, :128] + lines[:, 128:]).astype(BF16)

    q, _ = iotas(n_tile, n_rec)
    hits = q == rtile[...]
    hits_f = jnp.where(hits, 1.0, 0.0)
    q, n = iotas(n_rec, n_rec)
    rank = jnp.sum(hits_f * mm(hits_f.astype(BF16), onehot(q <= n)), axis=0, keepdims=True) - 1.0
    rank = rank.astype(I32)
    slot = rtile[...] * CAP + rank
    q, _ = iotas(n_tile * CAP, n_rec)
    send[...] = mm(onehot(q == slot), fixed).astype(BF16).reshape(n_tile, CAP, 128)
    q, _ = iotas(128, n_rec)
    place = onehot(q == rank)
    cell = rcell[...]
    dims = (((1,), (1,)), ((), ()))
    high = lax.dot_general((hits_f * (cell // 32 + 16).astype(F32)).astype(BF16), place, dims, preferred_element_type=F32)
    low = lax.dot_general((hits_f * lax.rem(cell, 32).astype(F32)).astype(BF16), place, dims, preferred_element_type=F32)
    send_c[...] = (high * 32.0 + low).reshape(n_tile, 1, 128)

    small[c, 0:1] = dw[...]
    small[c, 1:2] = eb[...]
    small[c, 2:4] = cb[...]

    pl.semaphore_wait(barrier, 2 * n_tile - 1 + 3)

    def send_cells(i, carry):
        d, k = far_first(i)
        remote(send_c.at[d], recv_c.at[c, k], s_cell, r_cell, dev(d, b, c)).start()
        return carry

    def send_rows(i, carry):
        d, k = far_first(i)
        remote(send.at[d], recv.at[c, k], s_rec, r_rec, dev(d, b, c)).start()
        remote(send.at[d], recv.at[c, k], s_rec, r_rec, dev(d, b, oc)).start()
        return carry

    pltpu.make_async_copy(send_c.at[t], recv_c.at[c, 0], r_cell).start()
    pltpu.make_async_copy(send.at[t], recv.at[c, 0], r_rec).start()
    lax.fori_loop(0, n_tile - 1, send_cells, 0)
    lax.fori_loop(0, n_tile - 1, send_rows, 0)
    remote(send.at[t], recv.at[c, 0], s_rec, r_rec, dev(t, b, oc)).start()

    par = [
        remote(ewh.at[c], ewh.at[c], s_par.at[0], r_par.at[0], dev(t, b, oc)),
        remote(small.at[c], small.at[c], s_par.at[1], r_par.at[1], dev(t, b, oc)),
    ]
    for p in par:
        p.start()
    n_w = cw.shape[1]
    quarter = n_w // 4
    near = [pl.ds(pl.multiple_of((2 * core + s) * quarter, 16), quarter) for s in range(2)]
    half = pl.ds(pl.multiple_of(2 * core * quarter, 16), 2 * quarter)
    parts, shares = [], []
    for layer in range(2):
        for s, to in enumerate((dev(t, b, oc), dev(zside, b, oc))):
            i = 2 * layer + s
            parts.append(remote(cw.at[layer, near[s]], wh.at[c, layer, near[s]], s_w.at[i], r_w.at[i], to))
        shares.append(remote(wh.at[oc, layer, half], wh.at[oc, layer, half], s_w2.at[layer], r_w2.at[layer], dev(sibling, b, c)))
    for p in parts:
        p.start()

    first = 34 * c
    sent = 2 + 30 * c
    lat_ok = jnp.logical_not(jnp.logical_or(jnp.logical_and(b == 0, c == 0), jnp.logical_and(b == n_band - 1, c == 1)))
    lat_ok = lat_ok.astype(I32)
    west_ok = (t > 0).astype(I32)
    east_ok = (t < n_tile - 1).astype(I32)

    q, n = iotas(MSG, NCELL)
    edge = 16 * q + jnp.where(q < EP, 0, jnp.where(q < 2 * EP, 1 - 16 * EP, jnp.where(q < 3 * EP, 14 - 32 * EP, 15 - 48 * EP)))
    m = q - 2 * SIDE
    side = jnp.where(m >= 16, 1, 0)
    m = m - 16 * side
    col = jnp.where(m >= 2, 1, 0)
    corner = (sent + m - 2 * col) * 16 + 14 * side + col
    corner = jnp.where(m < 4, corner, -1)
    col_sel[...] = onehot(n == jnp.where(q < 2 * SIDE, edge, corner))

    q, n = iotas(2 * SIDE, MSG)
    group = jnp.where(q >= EP, 1, 0) + jnp.where(q >= 2 * EP, 1, 0) + jnp.where(q >= 3 * EP, 1, 0)
    e = q - EP * group
    outer = jnp.logical_and(e >= first, e < first + 2)
    corner = 2 * SIDE + jnp.where(group >= 2, 16, 0) + jnp.where(jnp.logical_or(group == 1, group == 3), 2, 0) + e - first
    ok = jnp.where(group >= 2, east_ok, west_ok) * jnp.where(outer, lat_ok, 1)
    target = jnp.where(outer, corner, q)
    target = jnp.where(jnp.logical_and(ok > 0, e < EXT), target, -1)
    halo_sel[...] = onehot(n == target)

    q, n = iotas(NCELL, SIDE)
    ins_sel[...] = onehot(q == jnp.where(n < EP, 16 * n, 16 * (n - EP) + 15))
    q, n = iotas(SIDE, NCELL)
    own_sel[...] = onehot(n == jnp.where(q < EP, 16 * q, 16 * (q - EP) + 15))

    pltpu.make_async_copy(recv_c.at[c], recv_c.at[c], r_cell).wait()
    forward = remote(recv_c.at[c], recv_c.at[c], s_cell2, r_cell2, dev(t, b, oc))
    forward.start()
    parts[0].wait_recv()
    parts[1].wait_recv()
    shares[0].start()
    forward.wait_recv()
    q, n = iotas(n_tile, n_tile * CAP)
    spread = onehot(jnp.logical_and(n >= q * CAP, n < q * CAP + CAP))
    q, n = iotas(CAP, n_tile * CAP)
    mine = q == lax.rem(n, CAP)
    ids = []
    for s in range(2):
        code = recv_c[s].reshape(n_tile, 128)[:, :128]
        high = jnp.floor(code * (1.0 / 32.0))
        low = code - 32.0 * high
        dims = (((0,), (0,)), ((), ()))
        h = lax.dot_general(high.astype(BF16), spread, dims, preferred_element_type=F32)[:CAP]
        lo = lax.dot_general(low.astype(BF16), spread, dims, preferred_element_type=F32)[:CAP]
        ids.append(jnp.sum(jnp.where(mine, h * 32.0 + lo, 0.0), axis=0, keepdims=True))
    ids = jnp.concatenate(ids, axis=1)
    q, _ = iotas(NCELL, 2 * n_tile * CAP)
    hot = onehot(q == ids.astype(I32) - (512 + 16 * (HALF * c - 2)))

    for p in par:
        p.wait_recv()
    pltpu.make_async_copy(recv, recv, r_rec).wait()
    parts[2].wait_recv()
    parts[3].wait_recv()
    shares[1].start()

    values = recv[...].reshape(2 * n_tile * CAP, 128)
    sums = mm(hot, jnp.concatenate([values, jnp.ones_like(values)], axis=1))
    count = sums[:, 128:]
    averaged = (sums[:, :128] / jnp.maximum(count, 1.0)).astype(BF16)
    density = count / (count + 1.0)
    weights = jnp.concatenate([ewh[0], ewh[1]], axis=1)
    dens = jnp.concatenate([density * small[s, 0:1] + small[s, 1:2] for s in range(2)], axis=1)
    grid = (mm(averaged, weights) + dens).astype(BF16)
    field[...] = grid.reshape(EXT, LON_DEV, C)
    cols[...] = mm(col_sel[...], grid).astype(BF16)

    halo = [
        remote(field.at[pl.ds(sent, 2)], rows, s_halo.at[0], r_halo.at[0], dev(t, nb, oc)),
        remote(cols.at[pl.ds(0, SIDE)], msg.at[pl.ds(SIDE, SIDE)], s_halo.at[1], r_halo.at[1], dev(west, b, c)),
        remote(cols.at[pl.ds(SIDE, SIDE)], msg.at[pl.ds(0, SIDE)], s_halo.at[2], r_halo.at[2], dev(east, b, c)),
        remote(cols.at[pl.ds(2 * SIDE, 16)], msg.at[pl.ds(2 * SIDE + 16, 16)], s_halo.at[3], r_halo.at[3], dev(west, nb, oc)),
        remote(cols.at[pl.ds(2 * SIDE + 16, 16)], msg.at[pl.ds(2 * SIDE, 16)], s_halo.at[4], r_halo.at[4], dev(east, nb, oc)),
    ]
    for h in halo:
        h.start()
    shares[0].wait_recv()
    own_w.wait()
    halo[0].wait()
    field[pl.ds(first, 2)] = (rows[...].astype(F32) * lat_ok.astype(F32)).astype(BF16)
    for h in halo[1:]:
        h.wait()

    def weight(layer, i):
        part = pl.ds(i * 3 * C, 3 * C)
        return jnp.concatenate([wh[0, layer, part], wh[1, layer, part]], axis=1)

    def conv_bias(layer):
        return jnp.concatenate([small[0, 2 + layer : 3 + layer], small[1, 2 + layer : 3 + layer]], axis=1)

    def shifted(flat, insert):
        count = flat.shape[0]
        lon = lax.rem(lax.broadcasted_iota(I32, flat.shape, 0), LON_DEV)
        left = jnp.where(lon == 0, insert, pltpu.roll(flat, 1, 0)).astype(BF16)
        right = jnp.where(lon == LON_DEV - 1, insert, pltpu.roll(flat, count - 1, 0)).astype(BF16)
        return left.reshape(-1, LON_DEV, C), right.reshape(-1, LON_DEV, C)

    edges = mm(halo_sel[...], msg[...])
    edges_b = edges.astype(BF16)
    whole = field[...].reshape(NCELL, C)
    own = mm(own_sel[...], whole).astype(BF16)
    insert = mm(ins_sel[...], edges_b[EP : 3 * EP])
    left, right = shifted(whole.astype(F32), insert)
    x3[:, :, 0:C] = left
    x3[:, :, C : 2 * C] = field[...]
    x3[:, :, 2 * C :] = right
    xe[0:EP, 0:C] = edges_b[0:EP]
    xe[0:EP, C : 2 * C] = edges_b[EP : 2 * EP]
    xe[0:EP, 2 * C :] = own[0:EP]
    xe[EP:, 0:C] = own[EP:]
    xe[EP:, C : 2 * C] = edges_b[2 * EP : 3 * EP]
    xe[EP:, 2 * C :] = edges_b[3 * EP :]

    top_bad = jnp.logical_and(b == 0, c == 0).astype(I32)
    low_bad = jnp.logical_and(b == n_band - 1, c == 1).astype(I32)
    y = [mm(xe[...], weight(0, i)) for i in range(3)]
    y = pltpu.roll(y[0], 1, 0) + y[1] + pltpu.roll(y[2], SIDE - 1, 0) + conv_bias(0)
    q, _ = iotas(SIDE, C)
    e = jnp.where(q >= EP, q - EP, q)
    ok = jnp.where(q >= EP, east_ok, west_ok)
    keep = jnp.logical_and(ok > 0, jnp.logical_and(e >= 1 + top_bad, e <= EXT - 2 - low_bad))
    edge_out = jnp.where(keep, edges[EP : 3 * EP] + gelu(y), 0.0).astype(BF16)

    n_out = EXT - 2
    y = mm(x3[0:n_out].reshape(n_out * LON_DEV, 3 * C), weight(0, 0))
    y = y + mm(x3[1 : n_out + 1].reshape(n_out * LON_DEV, 3 * C), weight(0, 1))
    y = y + mm(x3[2 : n_out + 2].reshape(n_out * LON_DEV, 3 * C), weight(0, 2))
    y = gelu(y + conv_bias(0)) + field[1 : n_out + 1].reshape(n_out * LON_DEV, C).astype(F32)
    q, _ = iotas(n_out * LON_DEV, C)
    keep = jnp.logical_and(q >= LON_DEV * top_bad, q < LON_DEV * (n_out - low_bad))
    y = jnp.where(keep, y, 0.0)
    yb = y.astype(BF16)
    insert = mm(ins_sel[LON_DEV : LON_DEV * (n_out + 1), :], edge_out)
    left, right = shifted(yb.astype(F32), insert)
    x3g[:, :, 0:C] = left
    x3g[:, :, C : 2 * C] = yb.reshape(n_out, LON_DEV, C)
    x3g[:, :, 2 * C :] = right

    shares[1].wait_recv()
    chunk = 8
    n_chunk = HALF // chunk
    here = (t // HALF) == c

    def step(g, carry):
        far_z = jnp.where(c == 0, jnp.where(z_at == 1, 0, jnp.where(z_at == 3, 1, jnp.where(z_at == 0, 1, 0))), jnp.where(z_at == 3, 0, jnp.where(z_at == 1, 1, jnp.where(z_at == 2, 1, 0))))
        zz = lax.rem(far_z + g // 2, 2)
        at = (zz * 2 + lax.rem(x_at // 4 + 1 + g, 2)) * chunk
        y = mm(x3g[pl.ds(at, chunk)].reshape(chunk * LON_DEV, 3 * C), weight(1, 0))
        y = y + mm(x3g[pl.ds(at + 1, chunk)].reshape(chunk * LON_DEV, 3 * C), weight(1, 1))
        y = y + mm(x3g[pl.ds(at + 2, chunk)].reshape(chunk * LON_DEV, 3 * C), weight(1, 2))
        base = x3g[pl.ds(at + 1, chunk), :, C : 2 * C].reshape(chunk * LON_DEV, C).astype(F32)
        y = (gelu(y + conv_bias(1)) + base).astype(BF16)
        for s in range(2):
            res[s, pl.ds(at, chunk)] = y[:, 128 * s : 128 * s + 128].reshape(chunk, LON_DEV, 128)

        def deliver(k, carry):
            r = at + lax.rem(k + t, chunk)
            d = HALF * c + r
            mine = out.at[pl.ds(pl.multiple_of(t * LON_DEV, LON_DEV), LON_DEV)]
            remote(res.at[oc, r], mine, s_out, r_out, dev(d, b, oc)).start()

            @pl.when(d != t)
            def _():
                remote(res.at[c, r], mine, s_out, r_out, dev(d, b, c)).start()

            @pl.when(d == t)
            def _():
                pltpu.make_async_copy(res.at[c, r], mine, r_out).start()

            return carry

        lax.fori_loop(0, chunk, deliver, 0)
        return carry

    lax.fori_loop(0, n_chunk, step, 0)

    def sent_bytes(ref, sem):
        pltpu.make_async_copy(ref, ref, sem).wait()

    sent_bytes(send_c.at[pl.ds(0, n_tile - 1)], s_cell)
    sent_bytes(recv.at[0], s_rec)
    sent_bytes(recv.at[0, pl.ds(0, n_tile - 1)], s_rec)
    forward.wait_send()
    for p in par + parts + shares:
        p.wait_send()
    n_lon = n_tile * LON_DEV
    pl.when(here)(lambda: sent_bytes(out.at[pl.ds(0, n_lon - LON_DEV)], s_out))
    pl.when(jnp.logical_not(here))(lambda: sent_bytes(out, s_out))
    sent_bytes(out, r_out)


def local(n_tile, n_band, records, instrument, record_tile, record_cell, inst_gain, inst_bias, embed_weight, dens_weight, embed_bias, conv_weight, conv_bias):
    n_rec = records.shape[0]
    hbm = pl.BlockSpec(memory_space=pltpu.HBM)
    vmem = pl.BlockSpec(memory_space=pltpu.VMEM)
    dma, scratch = pltpu.SemaphoreType.DMA, pltpu.VMEM
    taps = 9 * C
    args = [
        pltpu.with_memory_space_constraint(x, pltpu.HBM)
        for x in (
            records,
            instrument.reshape(1, n_rec),
            record_tile.reshape(1, n_rec),
            record_cell.reshape(1, n_rec),
            inst_gain,
            inst_bias,
            embed_weight,
            dens_weight.reshape(1, -1),
            embed_bias.reshape(1, -1),
            conv_weight.reshape(2, taps, -1),
            conv_bias,
        )
    ]
    result = pl.pallas_call(
        functools.partial(kernel, n_tile, n_band),
        out_shape=jax.ShapeDtypeStruct((n_tile * LON_DEV, 128), BF16),
        in_specs=[hbm] * 11,
        out_specs=vmem,
        scratch_shapes=[
            scratch((n_rec, 128), BF16),
            scratch((1, n_rec), I32),
            scratch((1, n_rec), I32),
            scratch((1, n_rec), I32),
            scratch(inst_gain.shape, F32),
            scratch(inst_gain.shape, F32),
            scratch((1, 128), F32),
            scratch((1, 128), F32),
            scratch((2, 128), F32),
            scratch((n_tile, CAP, 128), BF16),
            scratch((n_tile, 1, 128), F32),
            scratch((2, n_tile, CAP, 128), BF16),
            scratch((2, n_tile, 1, 128), F32),
            scratch((2, 2, taps, 128), BF16),
            scratch((2, 128, 128), BF16),
            scratch((2, 8, 128), F32),
            scratch((EXT, LON_DEV, C), BF16),
            scratch((MSG, C), BF16),
            scratch((MSG, C), BF16),
            scratch((2, LON_DEV, C), BF16),
            scratch((EXT, LON_DEV, 3 * C), BF16),
            scratch((SIDE, 3 * C), BF16),
            scratch((EXT - 2, LON_DEV, 3 * C), BF16),
            scratch((2, HALF, LON_DEV, 128), BF16),
            scratch((2 * SIDE, MSG), BF16),
            scratch((NCELL, SIDE), BF16),
            scratch((MSG, NCELL), BF16),
            scratch((SIDE, NCELL), BF16),
            dma((11,)), dma, dma, dma, dma, dma, dma,
            dma((2,)), dma((2,)), dma((4,)), dma((4,)), dma((2,)), dma((2,)), dma((5,)), dma((5,)), dma, dma,
        ],
        compiler_params=pltpu.CompilerParams(
            collective_id=0, has_side_effects=True, vmem_limit_bytes=48 * 1024 * 1024
        ),
        name="encode",
    )(*args)
    return result[None, None]


def solution(mesh):
    in_specs = (
        P(("tile", "band", "chan"), None),
        P(("tile", "band", "chan")),
        P(("tile", "band", "chan"), None),
        P(("tile", "band", "chan")),
        P(),
        P(),
        P(None, "chan"),
        P("chan"),
        P("chan"),
        P(None, None, None, None, "chan"),
        P(None, "chan"),
    )
    return jax.shard_map(
        functools.partial(local, mesh.shape["tile"], mesh.shape["band"]),
        mesh=mesh,
        in_specs=in_specs,
        out_specs=P("tile", "band", None, "chan"),
        check_vma=False,
    )
```

```python
import functools
import math

import jax
import jax.numpy as jnp
from jax import lax
from jax.experimental import pallas as pl
from jax.experimental.pallas import tpu as pltpu
from jax.sharding import PartitionSpec as P

MESH = pl.DeviceIdType.MESH
F32, BF16, I32 = jnp.float32, jnp.bfloat16, jnp.int32
LAT_DEV, LON_DEV = 64, 16
HALF = LAT_DEV // 2
EXT = HALF + 4
EP = 48
CAP = 8
C = 256
SIDE = 2 * EP
MSG = 2 * SIDE + 32
NCELL = EXT * LON_DEV


def mm(a, b):
    return jnp.dot(a, b, preferred_element_type=F32)


def gelu(x):
    inner = math.sqrt(2.0 / math.pi) * (x + 0.044715 * (x * x * x))
    return 0.5 * x * (1.0 + jnp.tanh(inner))


def iotas(rows, cols):
    return lax.broadcasted_iota(I32, (rows, cols), 0), lax.broadcasted_iota(I32, (rows, cols), 1)


def onehot(mask):
    return jnp.where(mask, 1.0, 0.0).astype(BF16)


def thirds(x):
    a = x.astype(BF16).astype(F32)
    b = (x - a).astype(BF16).astype(F32)
    return [a, b, x - a - b]


def kernel(
    n_tile, n_band,
    rec_in, inst_in, rtile_in, rcell_in, gain_in, bias_in, ew_in, dw_in, eb_in, cw, cb_in,
    out,
    rec, inst, rtile, rcell, gain, bias, dw, eb, cb,
    send, send_c, recv, recv_c, wh, ewh, small,
    field, cols, msg, rows, x3, xe, x3g, res,
    halo_sel, ins_sel, col_sel, own_sel,
    s_loc, s_rec, r_rec, s_cell, r_cell, s_cell2, r_cell2,
    s_par, r_par, s_w, r_w, s_w2, r_w2, s_halo, r_halo, s_out, r_out,
):
    t, b, c = lax.axis_index("tile"), lax.axis_index("band"), lax.axis_index("chan")
    oc = 1 - c
    west, east = lax.rem(t + n_tile - 1, n_tile), lax.rem(t + 1, n_tile)
    nb = lax.rem(b + n_band - 1 + 2 * c, n_band)
    core = lax.rem(t, 2)
    sibling = t + 1 - 2 * core
    zside = lax.rem(t + n_tile - 16 + 32 * c, n_tile)
    halo_to = ((west, nb), (t, nb), (east, nb))

    def dev(tt, bb, cc):
        return {"tile": tt, "band": bb, "chan": cc}

    def remote(src, dst, ss, rs, to):
        return pltpu.make_async_remote_copy(
            src_ref=src, dst_ref=dst, send_sem=ss, recv_sem=rs, device_id=to, device_id_type=MESH
        )

    taken = [
        pltpu.make_async_copy(src, dst, s_loc.at[i])
        for i, (src, dst) in enumerate(
            [
                (rtile_in, rtile), (rcell_in, rcell), (inst_in, inst), (gain_in, gain), (bias_in, bias), (rec_in, rec),
                (dw_in, dw), (eb_in, eb), (cb_in, cb), (ew_in, ewh.at[c]), (cw, wh.at[c]),
            ]
        )
    ]
    for copy in taken:
        copy.start()
    own_w = taken[-1]

    barrier = pltpu.get_barrier_semaphore()

    def greet(tt, bb, cc):
        pl.semaphore_signal(barrier, inc=1, device_id=dev(tt, bb, cc), device_id_type=MESH)

    plane = 16
    z_at, in_plane = t // plane, lax.rem(t, plane)
    x_at = in_plane // 2

    n_z = n_tile // plane

    def far_first(act):
        def pair(dz, base, dx, both=True):
            x = x_at + dx
            x = jnp.where(x >= 8, x - 8, x)
            d = base + 2 * x
            k = (dz * 8 + dx) * 2
            act(d + 1 - core, k + 1)
            if both:
                act(d + core, k)

        for dz in (2, 1, 3, 0):
            z = z_at + dz
            base = jnp.where(z >= n_z, z - n_z, z) * plane

            def step(j, carry, dz=dz, base=base):
                pair(dz, base, 4 - j)
                pair(dz, base, 5 + j)
                return carry

            lax.fori_loop(0, 3, step, 0)
            pair(dz, base, 1)
            pair(dz, base, 0, both=dz != 0)

    def greet_band(d, k):
        greet(d, b, c)
        greet(d, b, oc)

    far_first(greet_band)
    for tt, bb in halo_to:
        greet(tt, bb, oc)
    greet(t, b, oc)


    for copy in taken[:-1]:
        copy.wait()

    n_inst = gain.shape[0]
    n_rec = rec.shape[0]
    q, _ = iotas(n_inst, n_rec)
    pick = jnp.where(q == inst[...], 1.0, 0.0)
    pick = jnp.concatenate([pick, pick, pick], axis=0).astype(BF16)
    table = jnp.concatenate(
        [jnp.concatenate(thirds(gain[...]), axis=0), jnp.concatenate(thirds(bias[...]), axis=0)],
        axis=1,
    ).astype(BF16)
    lines = lax.dot_general(pick, table, (((0,), (0,)), ((), ())), preferred_element_type=F32)
    fixed = (rec[...].astype(F32) * lines[:, :128] + lines[:, 128:]).astype(BF16)

    q, _ = iotas(n_tile, n_rec)
    hits = q == rtile[...]
    hits_f = jnp.where(hits, 1.0, 0.0)
    q, n = iotas(n_rec, n_rec)
    rank = jnp.sum(hits_f * mm(hits_f.astype(BF16), onehot(q <= n)), axis=0, keepdims=True) - 1.0
    rank = rank.astype(I32)
    slot = rtile[...] * CAP + rank
    q, _ = iotas(n_tile * CAP, n_rec)
    send[...] = mm(onehot(q == slot), fixed).astype(BF16).reshape(n_tile, CAP, 128)
    q, _ = iotas(128, n_rec)
    place = onehot(q == rank)
    cell = rcell[...]
    dims = (((1,), (1,)), ((), ()))
    high = lax.dot_general((hits_f * (cell // 32 + 16).astype(F32)).astype(BF16), place, dims, preferred_element_type=F32)
    low = lax.dot_general((hits_f * lax.rem(cell, 32).astype(F32)).astype(BF16), place, dims, preferred_element_type=F32)
    send_c[...] = (high * 32.0 + low).reshape(n_tile, 1, 128)

    small[c, 0:1] = dw[...]
    small[c, 1:2] = eb[...]
    small[c, 2:4] = cb[...]

    pl.semaphore_wait(barrier, 2 * n_tile - 1 + 3)

    def send_cells(d, k):
        remote(send_c.at[d], recv_c.at[c, k], s_cell, r_cell, dev(d, b, c)).start()

    def send_rows(d, k):
        remote(send.at[d], recv.at[c, k], s_rec, r_rec, dev(d, b, c)).start()
        remote(send.at[d], recv.at[c, k], s_rec, r_rec, dev(d, b, oc)).start()

    pltpu.make_async_copy(send_c.at[t], recv_c.at[c, 0], r_cell).start()
    pltpu.make_async_copy(send.at[t], recv.at[c, 0], r_rec).start()
    far_first(send_cells)
    far_first(send_rows)
    remote(send.at[t], recv.at[c, 0], s_rec, r_rec, dev(t, b, oc)).start()

    par = [
        remote(ewh.at[c], ewh.at[c], s_par.at[0], r_par.at[0], dev(t, b, oc)),
        remote(small.at[c], small.at[c], s_par.at[1], r_par.at[1], dev(t, b, oc)),
    ]
    for p in par:
        p.start()
    n_w = cw.shape[1]
    quarter = n_w // 4
    near = [pl.ds(pl.multiple_of((2 * core + s) * quarter, 16), quarter) for s in range(2)]
    half = pl.ds(pl.multiple_of(2 * core * quarter, 16), 2 * quarter)
    parts, shares = [], []
    for layer in range(2):
        for s, to in enumerate((dev(t, b, oc), dev(zside, b, oc))):
            i = 2 * layer + s
            parts.append(remote(cw.at[layer, near[s]], wh.at[c, layer, near[s]], s_w.at[i], r_w.at[i], to))
        shares.append(remote(wh.at[oc, layer, half], wh.at[oc, layer, half], s_w2.at[layer], r_w2.at[layer], dev(sibling, b, c)))
    parts[0].start()
    parts[1].start()

    first = 34 * c
    sent = 2 + 30 * c
    lat_ok = jnp.logical_not(jnp.logical_or(jnp.logical_and(b == 0, c == 0), jnp.logical_and(b == n_band - 1, c == 1)))
    lat_ok = lat_ok.astype(I32)
    west_ok = (t > 0).astype(I32)
    east_ok = (t < n_tile - 1).astype(I32)

    q, n = iotas(MSG, NCELL)
    edge = 16 * q + jnp.where(q < EP, 0, jnp.where(q < 2 * EP, 1 - 16 * EP, jnp.where(q < 3 * EP, 14 - 32 * EP, 15 - 48 * EP)))
    m = q - 2 * SIDE
    side = jnp.where(m >= 16, 1, 0)
    m = m - 16 * side
    col = jnp.where(m >= 2, 1, 0)
    corner = (sent + m - 2 * col) * 16 + 14 * side + col
    corner = jnp.where(m < 4, corner, -1)
    col_sel[...] = onehot(n == jnp.where(q < 2 * SIDE, edge, corner))

    q, n = iotas(2 * SIDE, MSG)
    group = jnp.where(q >= EP, 1, 0) + jnp.where(q >= 2 * EP, 1, 0) + jnp.where(q >= 3 * EP, 1, 0)
    e = q - EP * group
    outer = jnp.logical_and(e >= first, e < first + 2)
    corner = 2 * SIDE + jnp.where(group >= 2, 16, 0) + jnp.where(jnp.logical_or(group == 1, group == 3), 2, 0) + e - first
    ok = jnp.where(group >= 2, east_ok, west_ok) * jnp.where(outer, lat_ok, 1)
    target = jnp.where(outer, corner, q)
    target = jnp.where(jnp.logical_and(ok > 0, e < EXT), target, -1)
    halo_sel[...] = onehot(n == target)

    q, n = iotas(NCELL, SIDE)
    ins_sel[...] = onehot(q == jnp.where(n < EP, 16 * n, 16 * (n - EP) + 15))
    q, n = iotas(SIDE, NCELL)
    own_sel[...] = onehot(n == jnp.where(q < EP, 16 * q, 16 * (q - EP) + 15))

    pltpu.make_async_copy(recv_c.at[c], recv_c.at[c], r_cell).wait()
    forward = remote(recv_c.at[c], recv_c.at[c], s_cell2, r_cell2, dev(t, b, oc))
    forward.start()
    parts[0].wait_recv()
    parts[1].wait_recv()
    shares[0].start()
    forward.wait_recv()
    q, n = iotas(n_tile, n_tile * CAP)
    spread = onehot(jnp.logical_and(n >= q * CAP, n < q * CAP + CAP))
    q, n = iotas(CAP, n_tile * CAP)
    mine = q == lax.rem(n, CAP)
    ids = []
    for s in range(2):
        code = recv_c[s].reshape(n_tile, 128)[:, :128]
        high = jnp.floor(code * (1.0 / 32.0))
        low = code - 32.0 * high
        dims = (((0,), (0,)), ((), ()))
        h = lax.dot_general(high.astype(BF16), spread, dims, preferred_element_type=F32)[:CAP]
        lo = lax.dot_general(low.astype(BF16), spread, dims, preferred_element_type=F32)[:CAP]
        ids.append(jnp.sum(jnp.where(mine, h * 32.0 + lo, 0.0), axis=0, keepdims=True))
    ids = jnp.concatenate(ids, axis=1)
    q, _ = iotas(NCELL, 2 * n_tile * CAP)
    hot = onehot(q == ids.astype(I32) - (512 + 16 * (HALF * c - 2)))

    for p in par:
        p.wait_recv()
    pltpu.make_async_copy(recv, recv, r_rec).wait()
    parts[2].start()
    parts[3].start()

    values = recv[...].reshape(2 * n_tile * CAP, 128)
    sums = mm(hot, jnp.concatenate([values, jnp.ones_like(values)], axis=1))
    count = sums[:, 128:]
    averaged = (sums[:, :128] / jnp.maximum(count, 1.0)).astype(BF16)
    density = count / (count + 1.0)
    weights = jnp.concatenate([ewh[0], ewh[1]], axis=1)
    dens = jnp.concatenate([density * small[s, 0:1] + small[s, 1:2] for s in range(2)], axis=1)
    grid = (mm(averaged, weights) + dens).astype(BF16)
    field[...] = grid.reshape(EXT, LON_DEV, C)
    cols[...] = mm(col_sel[...], grid).astype(BF16)

    halo = [
        remote(field.at[pl.ds(sent, 2)], rows, s_halo.at[0], r_halo.at[0], dev(t, nb, oc)),
        remote(cols.at[pl.ds(0, SIDE)], msg.at[pl.ds(SIDE, SIDE)], s_halo.at[1], r_halo.at[1], dev(west, b, c)),
        remote(cols.at[pl.ds(SIDE, SIDE)], msg.at[pl.ds(0, SIDE)], s_halo.at[2], r_halo.at[2], dev(east, b, c)),
        remote(cols.at[pl.ds(2 * SIDE, 16)], msg.at[pl.ds(2 * SIDE + 16, 16)], s_halo.at[3], r_halo.at[3], dev(west, nb, oc)),
        remote(cols.at[pl.ds(2 * SIDE + 16, 16)], msg.at[pl.ds(2 * SIDE, 16)], s_halo.at[4], r_halo.at[4], dev(east, nb, oc)),
    ]
    for h in halo:
        h.start()
    shares[0].wait_recv()
    own_w.wait()
    halo[0].wait()
    field[pl.ds(first, 2)] = (rows[...].astype(F32) * lat_ok.astype(F32)).astype(BF16)
    for h in halo[1:]:
        h.wait()

    def weight(layer, i):
        part = pl.ds(i * 3 * C, 3 * C)
        return jnp.concatenate([wh[0, layer, part], wh[1, layer, part]], axis=1)

    def conv_bias(layer):
        return jnp.concatenate([small[0, 2 + layer : 3 + layer], small[1, 2 + layer : 3 + layer]], axis=1)

    def shifted(flat, insert):
        count = flat.shape[0]
        lon = lax.rem(lax.broadcasted_iota(I32, flat.shape, 0), LON_DEV)
        left = jnp.where(lon == 0, insert, pltpu.roll(flat, 1, 0)).astype(BF16)
        right = jnp.where(lon == LON_DEV - 1, insert, pltpu.roll(flat, count - 1, 0)).astype(BF16)
        return left.reshape(-1, LON_DEV, C), right.reshape(-1, LON_DEV, C)

    parts[2].wait_recv()
    parts[3].wait_recv()
    shares[1].start()
    edges = mm(halo_sel[...], msg[...])
    edges_b = edges.astype(BF16)
    whole = field[...].reshape(NCELL, C)
    own = mm(own_sel[...], whole).astype(BF16)
    insert = mm(ins_sel[...], edges_b[EP : 3 * EP])
    left, right = shifted(whole.astype(F32), insert)
    x3[:, :, 0:C] = left
    x3[:, :, C : 2 * C] = field[...]
    x3[:, :, 2 * C :] = right
    xe[0:EP, 0:C] = edges_b[0:EP]
    xe[0:EP, C : 2 * C] = edges_b[EP : 2 * EP]
    xe[0:EP, 2 * C :] = own[0:EP]
    xe[EP:, 0:C] = own[EP:]
    xe[EP:, C : 2 * C] = edges_b[2 * EP : 3 * EP]
    xe[EP:, 2 * C :] = edges_b[3 * EP :]

    top_bad = jnp.logical_and(b == 0, c == 0).astype(I32)
    low_bad = jnp.logical_and(b == n_band - 1, c == 1).astype(I32)
    y = [mm(xe[...], weight(0, i)) for i in range(3)]
    y = pltpu.roll(y[0], 1, 0) + y[1] + pltpu.roll(y[2], SIDE - 1, 0) + conv_bias(0)
    q, _ = iotas(SIDE, C)
    e = jnp.where(q >= EP, q - EP, q)
    ok = jnp.where(q >= EP, east_ok, west_ok)
    keep = jnp.logical_and(ok > 0, jnp.logical_and(e >= 1 + top_bad, e <= EXT - 2 - low_bad))
    edge_out = jnp.where(keep, edges[EP : 3 * EP] + gelu(y), 0.0).astype(BF16)

    n_out = EXT - 2
    y = mm(x3[0:n_out].reshape(n_out * LON_DEV, 3 * C), weight(0, 0))
    y = y + mm(x3[1 : n_out + 1].reshape(n_out * LON_DEV, 3 * C), weight(0, 1))
    y = y + mm(x3[2 : n_out + 2].reshape(n_out * LON_DEV, 3 * C), weight(0, 2))
    y = gelu(y + conv_bias(0)) + field[1 : n_out + 1].reshape(n_out * LON_DEV, C).astype(F32)
    q, _ = iotas(n_out * LON_DEV, C)
    keep = jnp.logical_and(q >= LON_DEV * top_bad, q < LON_DEV * (n_out - low_bad))
    y = jnp.where(keep, y, 0.0)
    yb = y.astype(BF16)
    insert = mm(ins_sel[LON_DEV : LON_DEV * (n_out + 1), :], edge_out)
    left, right = shifted(yb.astype(F32), insert)
    x3g[:, :, 0:C] = left
    x3g[:, :, C : 2 * C] = yb.reshape(n_out, LON_DEV, C)
    x3g[:, :, 2 * C :] = right

    shares[1].wait_recv()
    chunk = 8
    n_chunk = HALF // chunk
    here = (t // HALF) == c

    def step(g, carry):
        far_z = jnp.where(c == 0, jnp.where(z_at == 1, 0, jnp.where(z_at == 3, 1, jnp.where(z_at == 0, 1, 0))), jnp.where(z_at == 3, 0, jnp.where(z_at == 1, 1, jnp.where(z_at == 2, 1, 0))))
        zz = lax.rem(far_z + g // 2, 2)
        at = (zz * 2 + lax.rem(x_at // 4 + 1 + g, 2)) * chunk
        y = mm(x3g[pl.ds(at, chunk)].reshape(chunk * LON_DEV, 3 * C), weight(1, 0))
        y = y + mm(x3g[pl.ds(at + 1, chunk)].reshape(chunk * LON_DEV, 3 * C), weight(1, 1))
        y = y + mm(x3g[pl.ds(at + 2, chunk)].reshape(chunk * LON_DEV, 3 * C), weight(1, 2))
        base = x3g[pl.ds(at + 1, chunk), :, C : 2 * C].reshape(chunk * LON_DEV, C).astype(F32)
        y = (gelu(y + conv_bias(1)) + base).astype(BF16)
        for s in range(2):
            res[s, pl.ds(at, chunk)] = y[:, 128 * s : 128 * s + 128].reshape(chunk, LON_DEV, 128)

        def deliver(k, carry):
            r = at + lax.rem(k + t, chunk)
            d = HALF * c + r
            mine = out.at[pl.ds(pl.multiple_of(t * LON_DEV, LON_DEV), LON_DEV)]
            remote(res.at[oc, r], mine, s_out, r_out, dev(d, b, oc)).start()

            @pl.when(d != t)
            def _():
                remote(res.at[c, r], mine, s_out, r_out, dev(d, b, c)).start()

            @pl.when(d == t)
            def _():
                pltpu.make_async_copy(res.at[c, r], mine, r_out).start()

            return carry

        lax.fori_loop(0, chunk, deliver, 0)
        return carry

    lax.fori_loop(0, n_chunk, step, 0)

    def sent_bytes(ref, sem):
        pltpu.make_async_copy(ref, ref, sem).wait()

    sent_bytes(send_c.at[pl.ds(0, n_tile - 1)], s_cell)
    sent_bytes(recv.at[0], s_rec)
    sent_bytes(recv.at[0, pl.ds(0, n_tile - 1)], s_rec)
    forward.wait_send()
    for p in par + parts + shares:
        p.wait_send()
    n_lon = n_tile * LON_DEV
    pl.when(here)(lambda: sent_bytes(out.at[pl.ds(0, n_lon - LON_DEV)], s_out))
    pl.when(jnp.logical_not(here))(lambda: sent_bytes(out, s_out))
    sent_bytes(out, r_out)


def local(n_tile, n_band, records, instrument, record_tile, record_cell, inst_gain, inst_bias, embed_weight, dens_weight, embed_bias, conv_weight, conv_bias):
    n_rec = records.shape[0]
    hbm = pl.BlockSpec(memory_space=pltpu.HBM)
    vmem = pl.BlockSpec(memory_space=pltpu.VMEM)
    dma, scratch = pltpu.SemaphoreType.DMA, pltpu.VMEM
    taps = 9 * C
    args = [
        pltpu.with_memory_space_constraint(x, pltpu.HBM)
        for x in (
            records,
            instrument.reshape(1, n_rec),
            record_tile.reshape(1, n_rec),
            record_cell.reshape(1, n_rec),
            inst_gain,
            inst_bias,
            embed_weight,
            dens_weight.reshape(1, -1),
            embed_bias.reshape(1, -1),
            conv_weight.reshape(2, taps, -1),
            conv_bias,
        )
    ]
    result = pl.pallas_call(
        functools.partial(kernel, n_tile, n_band),
        out_shape=jax.ShapeDtypeStruct((n_tile * LON_DEV, 128), BF16),
        in_specs=[hbm] * 11,
        out_specs=vmem,
        scratch_shapes=[
            scratch((n_rec, 128), BF16),
            scratch((1, n_rec), I32),
            scratch((1, n_rec), I32),
            scratch((1, n_rec), I32),
            scratch(inst_gain.shape, F32),
            scratch(inst_gain.shape, F32),
            scratch((1, 128), F32),
            scratch((1, 128), F32),
            scratch((2, 128), F32),
            scratch((n_tile, CAP, 128), BF16),
            scratch((n_tile, 1, 128), F32),
            scratch((2, n_tile, CAP, 128), BF16),
            scratch((2, n_tile, 1, 128), F32),
            scratch((2, 2, taps, 128), BF16),
            scratch((2, 128, 128), BF16),
            scratch((2, 8, 128), F32),
            scratch((EXT, LON_DEV, C), BF16),
            scratch((MSG, C), BF16),
            scratch((MSG, C), BF16),
            scratch((2, LON_DEV, C), BF16),
            scratch((EXT, LON_DEV, 3 * C), BF16),
            scratch((SIDE, 3 * C), BF16),
            scratch((EXT - 2, LON_DEV, 3 * C), BF16),
            scratch((2, HALF, LON_DEV, 128), BF16),
            scratch((2 * SIDE, MSG), BF16),
            scratch((NCELL, SIDE), BF16),
            scratch((MSG, NCELL), BF16),
            scratch((SIDE, NCELL), BF16),
            dma((11,)), dma, dma, dma, dma, dma, dma,
            dma((2,)), dma((2,)), dma((4,)), dma((4,)), dma((2,)), dma((2,)), dma((5,)), dma((5,)), dma, dma,
        ],
        compiler_params=pltpu.CompilerParams(
            collective_id=0, has_side_effects=True, vmem_limit_bytes=48 * 1024 * 1024
        ),
        name="encode",
    )(*args)
    return result[None, None]


def solution(mesh):
    in_specs = (
        P(("tile", "band", "chan"), None),
        P(("tile", "band", "chan")),
        P(("tile", "band", "chan"), None),
        P(("tile", "band", "chan")),
        P(),
        P(),
        P(None, "chan"),
        P("chan"),
        P("chan"),
        P(None, None, None, None, "chan"),
        P(None, "chan"),
    )
    return jax.shard_map(
        functools.partial(local, mesh.shape["tile"], mesh.shape["band"]),
        mesh=mesh,
        in_specs=in_specs,
        out_specs=P("tile", "band", None, "chan"),
        check_vma=False,
    )
```

```python
import functools
import math

import jax
import jax.numpy as jnp
from jax import lax
from jax.experimental import pallas as pl
from jax.experimental.pallas import tpu as pltpu
from jax.sharding import PartitionSpec as P

MESH = pl.DeviceIdType.MESH
F32, BF16, I32 = jnp.float32, jnp.bfloat16, jnp.int32
LAT_DEV, LON_DEV = 64, 16
HALF = LAT_DEV // 2
EXT = HALF + 4
EP = 48
CAP = 8
C = 256
SIDE = 2 * EP
MSG = 2 * SIDE + 32
NCELL = EXT * LON_DEV


def mm(a, b):
    return jnp.dot(a, b, preferred_element_type=F32)


def gelu(x):
    inner = math.sqrt(2.0 / math.pi) * (x + 0.044715 * (x * x * x))
    return 0.5 * x * (1.0 + jnp.tanh(inner))


def iotas(rows, cols):
    return lax.broadcasted_iota(I32, (rows, cols), 0), lax.broadcasted_iota(I32, (rows, cols), 1)


def onehot(mask):
    return jnp.where(mask, 1.0, 0.0).astype(BF16)


def thirds(x):
    a = x.astype(BF16).astype(F32)
    b = (x - a).astype(BF16).astype(F32)
    return [a, b, x - a - b]


def kernel(
    n_tile, n_band,
    rec_in, inst_in, rtile_in, rcell_in, gain_in, bias_in, ew_in, dw_in, eb_in, cw, cb_in,
    out,
    rec, inst, rtile, rcell, gain, bias, dw, eb, cb,
    send, send_c, recv, recv_c, wh, ewh, small,
    field, cols, msg, rows, x3, xe, x3g, res,
    halo_sel, ins_sel, col_sel, own_sel,
    s_loc, s_rec, r_rec, s_cell, r_cell, s_cell2, r_cell2,
    s_par, r_par, s_w, r_w, s_w2, r_w2, s_halo, r_halo, s_out, r_out,
):
    t, b, c = lax.axis_index("tile"), lax.axis_index("band"), lax.axis_index("chan")
    oc = 1 - c
    west, east = lax.rem(t + n_tile - 1, n_tile), lax.rem(t + 1, n_tile)
    nb = lax.rem(b + n_band - 1 + 2 * c, n_band)
    core = lax.rem(t, 2)
    sibling = t + 1 - 2 * core
    zside = lax.rem(t + n_tile - 16 + 32 * c, n_tile)
    halo_to = ((west, nb), (t, nb), (east, nb))

    def dev(tt, bb, cc):
        return {"tile": tt, "band": bb, "chan": cc}

    def remote(src, dst, ss, rs, to):
        return pltpu.make_async_remote_copy(
            src_ref=src, dst_ref=dst, send_sem=ss, recv_sem=rs, device_id=to, device_id_type=MESH
        )

    taken = [
        pltpu.make_async_copy(src, dst, s_loc.at[i])
        for i, (src, dst) in enumerate(
            [
                (rtile_in, rtile), (rcell_in, rcell), (inst_in, inst), (gain_in, gain), (bias_in, bias), (rec_in, rec),
                (dw_in, dw), (eb_in, eb), (cb_in, cb), (ew_in, ewh.at[c]), (cw, wh.at[c]),
            ]
        )
    ]
    for copy in taken:
        copy.start()
    own_w = taken[-1]

    barrier = pltpu.get_barrier_semaphore()

    def greet(tt, bb, cc):
        pl.semaphore_signal(barrier, inc=1, device_id=dev(tt, bb, cc), device_id_type=MESH)

    plane = 16
    z_at, in_plane = t // plane, lax.rem(t, plane)
    x_at = in_plane // 2

    n_z = n_tile // plane

    def far_first(act):
        def pair(dz, base, dx, both=True):
            x = x_at + dx
            x = jnp.where(x >= 8, x - 8, x)
            d = base + 2 * x
            k = (dz * 8 + dx) * 2
            act(d + 1 - core, k + 1)
            if both:
                act(d + core, k)

        for dz in (2, 1, 3, 0):
            z = z_at + dz
            base = jnp.where(z >= n_z, z - n_z, z) * plane

            def step(j, carry, dz=dz, base=base):
                pair(dz, base, 4 - j)
                pair(dz, base, 5 + j)
                return carry

            lax.fori_loop(0, 3, step, 0)
            pair(dz, base, 1)
            pair(dz, base, 0, both=dz != 0)

    def greet_band(d, k):
        greet(d, b, c)
        greet(d, b, oc)

    far_first(greet_band)
    for tt, bb in halo_to:
        greet(tt, bb, oc)
    greet(t, b, oc)


    for copy in taken[:-1]:
        copy.wait()

    n_inst = gain.shape[0]
    n_rec = rec.shape[0]
    q, _ = iotas(n_inst, n_rec)
    pick = jnp.where(q == inst[...], 1.0, 0.0)
    pick = jnp.concatenate([pick, pick, pick], axis=0).astype(BF16)
    table = jnp.concatenate(
        [jnp.concatenate(thirds(gain[...]), axis=0), jnp.concatenate(thirds(bias[...]), axis=0)],
        axis=1,
    ).astype(BF16)
    lines = lax.dot_general(pick, table, (((0,), (0,)), ((), ())), preferred_element_type=F32)
    fixed = (rec[...].astype(F32) * lines[:, :128] + lines[:, 128:]).astype(BF16)

    q, _ = iotas(n_tile, n_rec)
    hits = q == rtile[...]
    hits_f = jnp.where(hits, 1.0, 0.0)
    q, n = iotas(n_rec, n_rec)
    rank = jnp.sum(hits_f * mm(hits_f.astype(BF16), onehot(q <= n)), axis=0, keepdims=True) - 1.0
    rank = rank.astype(I32)
    slot = rtile[...] * CAP + rank
    q, _ = iotas(n_tile * CAP, n_rec)
    send[...] = mm(onehot(q == slot), fixed).astype(BF16).reshape(n_tile, CAP, 128)
    q, _ = iotas(128, n_rec)
    place = onehot(q == rank)
    cell = rcell[...]
    dims = (((1,), (1,)), ((), ()))
    high = lax.dot_general((hits_f * (cell // 32 + 16).astype(F32)).astype(BF16), place, dims, preferred_element_type=F32)
    low = lax.dot_general((hits_f * lax.rem(cell, 32).astype(F32)).astype(BF16), place, dims, preferred_element_type=F32)
    send_c[...] = (high * 32.0 + low).reshape(n_tile, 1, 128)

    small[c, 0:1] = dw[...]
    small[c, 1:2] = eb[...]
    small[c, 2:4] = cb[...]

    pl.semaphore_wait(barrier, 2 * n_tile - 1 + 3)

    def send_cells(d, k):
        remote(send_c.at[d], recv_c.at[c, k], s_cell, r_cell, dev(d, b, c)).start()

    def send_rows(d, k):
        remote(send.at[d], recv.at[c, k], s_rec, r_rec, dev(d, b, c)).start()
        remote(send.at[d], recv.at[c, k], s_rec, r_rec, dev(d, b, oc)).start()

    pltpu.make_async_copy(send_c.at[t], recv_c.at[c, 0], r_cell).start()
    pltpu.make_async_copy(send.at[t], recv.at[c, 0], r_rec).start()
    far_first(send_cells)
    far_first(send_rows)
    remote(send.at[t], recv.at[c, 0], s_rec, r_rec, dev(t, b, oc)).start()

    par = [
        remote(ewh.at[c], ewh.at[c], s_par.at[0], r_par.at[0], dev(t, b, oc)),
        remote(small.at[c], small.at[c], s_par.at[1], r_par.at[1], dev(t, b, oc)),
    ]
    for p in par:
        p.start()
    n_w = cw.shape[1]
    quarter = n_w // 4
    near = [pl.ds(pl.multiple_of((2 * core + s) * quarter, 16), quarter) for s in range(2)]
    half = pl.ds(pl.multiple_of(2 * core * quarter, 16), 2 * quarter)
    parts, shares = [], []
    for layer in range(2):
        for s, to in enumerate((dev(t, b, oc), dev(zside, b, oc))):
            i = 2 * layer + s
            parts.append(remote(cw.at[layer, near[s]], wh.at[c, layer, near[s]], s_w.at[i], r_w.at[i], to))
        shares.append(remote(wh.at[oc, layer, half], wh.at[oc, layer, half], s_w2.at[layer], r_w2.at[layer], dev(sibling, b, c)))
    parts[0].start()
    parts[1].start()

    first = 34 * c
    sent = 2 + 30 * c
    lat_ok = jnp.logical_not(jnp.logical_or(jnp.logical_and(b == 0, c == 0), jnp.logical_and(b == n_band - 1, c == 1)))
    lat_ok = lat_ok.astype(I32)
    west_ok = (t > 0).astype(I32)
    east_ok = (t < n_tile - 1).astype(I32)

    q, n = iotas(MSG, NCELL)
    edge = 16 * q + jnp.where(q < EP, 0, jnp.where(q < 2 * EP, 1 - 16 * EP, jnp.where(q < 3 * EP, 14 - 32 * EP, 15 - 48 * EP)))
    m = q - 2 * SIDE
    side = jnp.where(m >= 16, 1, 0)
    m = m - 16 * side
    col = jnp.where(m >= 2, 1, 0)
    corner = (sent + m - 2 * col) * 16 + 14 * side + col
    corner = jnp.where(m < 4, corner, -1)
    col_sel[...] = onehot(n == jnp.where(q < 2 * SIDE, edge, corner))

    q, n = iotas(2 * SIDE, MSG)
    group = jnp.where(q >= EP, 1, 0) + jnp.where(q >= 2 * EP, 1, 0) + jnp.where(q >= 3 * EP, 1, 0)
    e = q - EP * group
    outer = jnp.logical_and(e >= first, e < first + 2)
    corner = 2 * SIDE + jnp.where(group >= 2, 16, 0) + jnp.where(jnp.logical_or(group == 1, group == 3), 2, 0) + e - first
    ok = jnp.where(group >= 2, east_ok, west_ok) * jnp.where(outer, lat_ok, 1)
    target = jnp.where(outer, corner, q)
    target = jnp.where(jnp.logical_and(ok > 0, e < EXT), target, -1)
    halo_sel[...] = onehot(n == target)

    q, n = iotas(NCELL, SIDE)
    ins_sel[...] = onehot(q == jnp.where(n < EP, 16 * n, 16 * (n - EP) + 15))
    q, n = iotas(SIDE, NCELL)
    own_sel[...] = onehot(n == jnp.where(q < EP, 16 * q, 16 * (q - EP) + 15))

    pltpu.make_async_copy(recv_c.at[c], recv_c.at[c], r_cell).wait()
    forward = remote(recv_c.at[c], recv_c.at[c], s_cell2, r_cell2, dev(t, b, oc))
    forward.start()
    parts[0].wait_recv()
    parts[1].wait_recv()
    shares[0].start()
    forward.wait_recv()
    q, n = iotas(n_tile, n_tile * CAP)
    spread = onehot(jnp.logical_and(n >= q * CAP, n < q * CAP + CAP))
    q, n = iotas(CAP, n_tile * CAP)
    mine = q == lax.rem(n, CAP)
    ids = []
    for s in range(2):
        code = recv_c[s].reshape(n_tile, 128)[:, :128]
        high = jnp.floor(code * (1.0 / 32.0))
        low = code - 32.0 * high
        dims = (((0,), (0,)), ((), ()))
        h = lax.dot_general(high.astype(BF16), spread, dims, preferred_element_type=F32)[:CAP]
        lo = lax.dot_general(low.astype(BF16), spread, dims, preferred_element_type=F32)[:CAP]
        ids.append(jnp.sum(jnp.where(mine, h * 32.0 + lo, 0.0), axis=0, keepdims=True))
    ids = jnp.concatenate(ids, axis=1)
    q, _ = iotas(NCELL, 2 * n_tile * CAP)
    hot = onehot(q == ids.astype(I32) - (512 + 16 * (HALF * c - 2)))

    for p in par:
        p.wait_recv()
    pltpu.make_async_copy(recv, recv, r_rec).wait()
    parts[2].start()
    parts[3].start()

    values = recv[...].reshape(2 * n_tile * CAP, 128)
    sums = mm(hot, jnp.concatenate([values, jnp.ones_like(values)], axis=1))
    count = sums[:, 128:]
    averaged = (sums[:, :128] / jnp.maximum(count, 1.0)).astype(BF16)
    density = count / (count + 1.0)
    weights = jnp.concatenate([ewh[0], ewh[1]], axis=1)
    dens = jnp.concatenate([density * small[s, 0:1] + small[s, 1:2] for s in range(2)], axis=1)
    grid = (mm(averaged, weights) + dens).astype(BF16)
    field[...] = grid.reshape(EXT, LON_DEV, C)
    cols[...] = mm(col_sel[...], grid).astype(BF16)

    halo = [
        remote(field.at[pl.ds(sent, 2)], rows, s_halo.at[0], r_halo.at[0], dev(t, nb, oc)),
        remote(cols.at[pl.ds(0, SIDE)], msg.at[pl.ds(SIDE, SIDE)], s_halo.at[1], r_halo.at[1], dev(west, b, c)),
        remote(cols.at[pl.ds(SIDE, SIDE)], msg.at[pl.ds(0, SIDE)], s_halo.at[2], r_halo.at[2], dev(east, b, c)),
        remote(cols.at[pl.ds(2 * SIDE, 16)], msg.at[pl.ds(2 * SIDE + 16, 16)], s_halo.at[3], r_halo.at[3], dev(west, nb, oc)),
        remote(cols.at[pl.ds(2 * SIDE + 16, 16)], msg.at[pl.ds(2 * SIDE, 16)], s_halo.at[4], r_halo.at[4], dev(east, nb, oc)),
    ]
    for h in halo:
        h.start()
    shares[0].wait_recv()
    own_w.wait()
    halo[0].wait()
    field[pl.ds(first, 2)] = (rows[...].astype(F32) * lat_ok.astype(F32)).astype(BF16)
    for h in halo[1:]:
        h.wait()
    parts[2].wait_recv()
    parts[3].wait_recv()
    shares[1].start()

    def weight(layer, i):
        part = pl.ds(i * 3 * C, 3 * C)
        return jnp.concatenate([wh[0, layer, part], wh[1, layer, part]], axis=1)

    def conv_bias(layer):
        return jnp.concatenate([small[0, 2 + layer : 3 + layer], small[1, 2 + layer : 3 + layer]], axis=1)

    def shifted(flat, insert):
        count = flat.shape[0]
        lon = lax.rem(lax.broadcasted_iota(I32, flat.shape, 0), LON_DEV)
        left = jnp.where(lon == 0, insert, pltpu.roll(flat, 1, 0)).astype(BF16)
        right = jnp.where(lon == LON_DEV - 1, insert, pltpu.roll(flat, count - 1, 0)).astype(BF16)
        return left.reshape(-1, LON_DEV, C), right.reshape(-1, LON_DEV, C)

    edges = mm(halo_sel[...], msg[...])
    edges_b = edges.astype(BF16)
    whole = field[...].reshape(NCELL, C)
    own = mm(own_sel[...], whole).astype(BF16)
    insert = mm(ins_sel[...], edges_b[EP : 3 * EP])
    left, right = shifted(whole.astype(F32), insert)
    x3[:, :, 0:C] = left
    x3[:, :, C : 2 * C] = field[...]
    x3[:, :, 2 * C :] = right
    xe[0:EP, 0:C] = edges_b[0:EP]
    xe[0:EP, C : 2 * C] = edges_b[EP : 2 * EP]
    xe[0:EP, 2 * C :] = own[0:EP]
    xe[EP:, 0:C] = own[EP:]
    xe[EP:, C : 2 * C] = edges_b[2 * EP : 3 * EP]
    xe[EP:, 2 * C :] = edges_b[3 * EP :]

    top_bad = jnp.logical_and(b == 0, c == 0).astype(I32)
    low_bad = jnp.logical_and(b == n_band - 1, c == 1).astype(I32)
    y = [mm(xe[...], weight(0, i)) for i in range(3)]
    y = pltpu.roll(y[0], 1, 0) + y[1] + pltpu.roll(y[2], SIDE - 1, 0) + conv_bias(0)
    q, _ = iotas(SIDE, C)
    e = jnp.where(q >= EP, q - EP, q)
    ok = jnp.where(q >= EP, east_ok, west_ok)
    keep = jnp.logical_and(ok > 0, jnp.logical_and(e >= 1 + top_bad, e <= EXT - 2 - low_bad))
    edge_out = jnp.where(keep, edges[EP : 3 * EP] + gelu(y), 0.0).astype(BF16)

    n_out = EXT - 2
    y = mm(x3[0:n_out].reshape(n_out * LON_DEV, 3 * C), weight(0, 0))
    y = y + mm(x3[1 : n_out + 1].reshape(n_out * LON_DEV, 3 * C), weight(0, 1))
    y = y + mm(x3[2 : n_out + 2].reshape(n_out * LON_DEV, 3 * C), weight(0, 2))
    y = gelu(y + conv_bias(0)) + field[1 : n_out + 1].reshape(n_out * LON_DEV, C).astype(F32)
    q, _ = iotas(n_out * LON_DEV, C)
    keep = jnp.logical_and(q >= LON_DEV * top_bad, q < LON_DEV * (n_out - low_bad))
    y = jnp.where(keep, y, 0.0)
    yb = y.astype(BF16)
    insert = mm(ins_sel[LON_DEV : LON_DEV * (n_out + 1), :], edge_out)
    left, right = shifted(yb.astype(F32), insert)
    x3g[:, :, 0:C] = left
    x3g[:, :, C : 2 * C] = yb.reshape(n_out, LON_DEV, C)
    x3g[:, :, 2 * C :] = right

    shares[1].wait_recv()
    chunk = 8
    n_chunk = HALF // chunk
    here = (t // HALF) == c
    t_low, t_row = lax.rem(t, chunk), lax.rem(t, HALF)

    far_z = jnp.where(c == 0, jnp.where(z_at == 1, 0, jnp.where(z_at == 3, 1, jnp.where(z_at == 0, 1, 0))), jnp.where(z_at == 3, 0, jnp.where(z_at == 1, 1, jnp.where(z_at == 2, 1, 0))))

    def step(g, carry):
        zz = lax.rem(far_z + g // 2, 2)
        at = (zz * 2 + lax.rem(x_at // 4 + 1 + g, 2)) * chunk
        y = mm(x3g[pl.ds(at, chunk)].reshape(chunk * LON_DEV, 3 * C), weight(1, 0))
        y = y + mm(x3g[pl.ds(at + 1, chunk)].reshape(chunk * LON_DEV, 3 * C), weight(1, 1))
        y = y + mm(x3g[pl.ds(at + 2, chunk)].reshape(chunk * LON_DEV, 3 * C), weight(1, 2))
        base = x3g[pl.ds(at + 1, chunk), :, C : 2 * C].reshape(chunk * LON_DEV, C).astype(F32)
        y = (gelu(y + conv_bias(1)) + base).astype(BF16)
        for s in range(2):
            res[s, pl.ds(at, chunk)] = y[:, 128 * s : 128 * s + 128].reshape(chunk, LON_DEV, 128)

        mine = out.at[pl.ds(pl.multiple_of(t * LON_DEV, LON_DEV), LON_DEV)]

        def row(k):
            r = k + t_low
            return at + jnp.where(r >= chunk, r - chunk, r)

        def deliver(r, cc):
            remote(res.at[cc, r], mine, s_out, r_out, dev(HALF * c + r, b, cc)).start()

        stays = jnp.logical_and(here, jnp.logical_and(at <= t_row, t_row < at + chunk))

        @pl.when(jnp.logical_not(stays))
        def _():
            for k in range(chunk):
                deliver(row(k), oc)
                deliver(row(k), c)

        @pl.when(stays)
        def _():
            pltpu.make_async_copy(res.at[c, t_row], mine, r_out).start()
            deliver(row(0), oc)
            for k in range(1, chunk):
                deliver(row(k), oc)
                deliver(row(k), c)

        return carry

    lax.fori_loop(0, n_chunk, step, 0)

    def sent_bytes(ref, sem):
        pltpu.make_async_copy(ref, ref, sem).wait()

    sent_bytes(send_c.at[pl.ds(0, n_tile - 1)], s_cell)
    sent_bytes(recv.at[0], s_rec)
    sent_bytes(recv.at[0, pl.ds(0, n_tile - 1)], s_rec)
    forward.wait_send()
    for p in par + parts + shares:
        p.wait_send()
    n_lon = n_tile * LON_DEV
    pl.when(here)(lambda: sent_bytes(out.at[pl.ds(0, n_lon - LON_DEV)], s_out))
    pl.when(jnp.logical_not(here))(lambda: sent_bytes(out, s_out))
    sent_bytes(out, r_out)


def local(n_tile, n_band, records, instrument, record_tile, record_cell, inst_gain, inst_bias, embed_weight, dens_weight, embed_bias, conv_weight, conv_bias):
    n_rec = records.shape[0]
    hbm = pl.BlockSpec(memory_space=pltpu.HBM)
    vmem = pl.BlockSpec(memory_space=pltpu.VMEM)
    dma, scratch = pltpu.SemaphoreType.DMA, pltpu.VMEM
    taps = 9 * C
    args = [
        pltpu.with_memory_space_constraint(x, pltpu.HBM)
        for x in (
            records,
            instrument.reshape(1, n_rec),
            record_tile.reshape(1, n_rec),
            record_cell.reshape(1, n_rec),
            inst_gain,
            inst_bias,
            embed_weight,
            dens_weight.reshape(1, -1),
            embed_bias.reshape(1, -1),
            conv_weight.reshape(2, taps, -1),
            conv_bias,
        )
    ]
    result = pl.pallas_call(
        functools.partial(kernel, n_tile, n_band),
        out_shape=jax.ShapeDtypeStruct((n_tile * LON_DEV, 128), BF16),
        in_specs=[hbm] * 11,
        out_specs=vmem,
        scratch_shapes=[
            scratch((n_rec, 128), BF16),
            scratch((1, n_rec), I32),
            scratch((1, n_rec), I32),
            scratch((1, n_rec), I32),
            scratch(inst_gain.shape, F32),
            scratch(inst_gain.shape, F32),
            scratch((1, 128), F32),
            scratch((1, 128), F32),
            scratch((2, 128), F32),
            scratch((n_tile, CAP, 128), BF16),
            scratch((n_tile, 1, 128), F32),
            scratch((2, n_tile, CAP, 128), BF16),
            scratch((2, n_tile, 1, 128), F32),
            scratch((2, 2, taps, 128), BF16),
            scratch((2, 128, 128), BF16),
            scratch((2, 8, 128), F32),
            scratch((EXT, LON_DEV, C), BF16),
            scratch((MSG, C), BF16),
            scratch((MSG, C), BF16),
            scratch((2, LON_DEV, C), BF16),
            scratch((EXT, LON_DEV, 3 * C), BF16),
            scratch((SIDE, 3 * C), BF16),
            scratch((EXT - 2, LON_DEV, 3 * C), BF16),
            scratch((2, HALF, LON_DEV, 128), BF16),
            scratch((2 * SIDE, MSG), BF16),
            scratch((NCELL, SIDE), BF16),
            scratch((MSG, NCELL), BF16),
            scratch((SIDE, NCELL), BF16),
            dma((11,)), dma, dma, dma, dma, dma, dma,
            dma((2,)), dma((2,)), dma((4,)), dma((4,)), dma((2,)), dma((2,)), dma((5,)), dma((5,)), dma, dma,
        ],
        compiler_params=pltpu.CompilerParams(
            collective_id=0, has_side_effects=True, vmem_limit_bytes=48 * 1024 * 1024
        ),
        name="encode",
    )(*args)
    return result[None, None]


def solution(mesh):
    in_specs = (
        P(("tile", "band", "chan"), None),
        P(("tile", "band", "chan")),
        P(("tile", "band", "chan"), None),
        P(("tile", "band", "chan")),
        P(),
        P(),
        P(None, "chan"),
        P("chan"),
        P("chan"),
        P(None, None, None, None, "chan"),
        P(None, "chan"),
    )
    return jax.shard_map(
        functools.partial(local, mesh.shape["tile"], mesh.shape["band"]),
        mesh=mesh,
        in_specs=in_specs,
        out_specs=P("tile", "band", None, "chan"),
        check_vma=False,
    )
```
